256 devices in a mesh: tier: 8 (over z), aux: 32 (over y, x, core).
Axes of the slice: x: 4, y: 4, z: 8, core: 2. Of those that a mesh axis runs over, the one named last changes fastest.
Arguments:
- section_state: float32 [2048, 18432], P(('tier', 'aux')), may hold values from -6 to 6
- coupling: float32 [96, 96], replicated, may hold values from -0.625 to 0.625
- site_energy: float32 [96], replicated, may hold values from -1 to 1
- bath_rate: float32 [96], replicated, may hold values from 0.3 to 3
- bath_strength: float32 [96], replicated, may hold values from 0.1 to 1
- bath_of_site: int32 [96], replicated, may hold values from 0 to 95, each once
- quanta: int32 [2048, 4], P(('tier', 'aux')), may hold values from -1 to 95, as said below
- send_list: int32 [256, 128], P(('tier', 'aux')), may hold values from -1 to 31, as said below
- dest_slot: int32 [256, 128], P(('tier', 'aux')), may hold values from 0 to 7
Outputs:
- derivative: float32 [2048, 18432], P(('tier', 'aux'))
The draws below stay inside these ranges and needn't reach their ends.
Inputs may be any that keep to these rules, and one draw needn't show every extreme that they name: Row a lists the sites of auxiliary a's quanta, 1 to 4 of them with repeats allowed, in ascending order, then -1 in the empty places. `send_list`: entry [d, l] is slot * 4 + place for an auxiliary slot of device d, or -1. The first place of every distinct site of every auxiliary stands in exactly one lane of its device, and no other place stands anywhere. On every device the 2 lanes of group 0 towards one aux index are all used.
All inputs are finite; a program needn't handle non-finite values.
Results may differ from the reference program's by a relative error of at most 0.00005.
Values sent between devices are 32-bit elements; how exact they have to be, the bound alone decides.
A program may use at most 64 MiB of HBM per device.

```python
import math
import jax
import jax.numpy as jnp
from jax import lax

SITES = 96
DEPTH = 4
AUX_DEV = 8
PEERS = 32
HOLDERS = 256
AUX = 2048
CAP = 2
LANES = 128


def edge_tables(key):
    base = jax.random.fold_in(key, 41)
    tier_key, site_key, peer_key, order_key = jax.random.split(base, 4)
    tier_counts = jax.random.randint(tier_key, (AUX,), 1, DEPTH + 1)
    places = jnp.arange(DEPTH)
    drawn_sites = jax.random.randint(site_key, (AUX, DEPTH), 0, SITES)
    drawn_sites = jnp.where(places[None, :] < tier_counts[:, None], drawn_sites, SITES)
    ordered = jnp.sort(drawn_sites, axis=1)
    quanta = jnp.where(ordered < SITES, ordered, -1).astype(jnp.int32)
    previous = jnp.concatenate([jnp.full((AUX, 1), -2, jnp.int32), quanta[:, :-1]], axis=1)
    firsts = (quanta >= 0) & (quanta != previous)
    per_holder = firsts.reshape(HOLDERS, AUX_DEV * DEPTH)
    edge_rank = jnp.cumsum(per_holder.astype(jnp.int32), axis=1) - 1
    first_peer = jax.random.randint(peer_key, (HOLDERS, 1), 0, PEERS)
    first_lane = first_peer * CAP
    shuffles = jax.vmap(lambda subkey: jax.random.permutation(subkey, LANES - CAP))(jax.random.split(order_key, HOLDERS))
    other_lanes = jnp.take_along_axis(shuffles, jnp.clip(edge_rank - CAP, 0, LANES - CAP - 1), axis=1)
    other_lanes = jnp.where(other_lanes >= first_lane, other_lanes + CAP, other_lanes)
    lane_of_edge = jnp.where(edge_rank < CAP, first_lane + edge_rank, other_lanes)
    lane_of_edge = jnp.where(per_holder, lane_of_edge, LANES).astype(jnp.int32)
    edge_ids = jnp.broadcast_to(jnp.arange(AUX_DEV * DEPTH, dtype=jnp.int32)[None, :], (HOLDERS, AUX_DEV * DEPTH))
    holder_ids = jnp.broadcast_to(jnp.arange(HOLDERS, dtype=jnp.int32)[:, None], (HOLDERS, AUX_DEV * DEPTH))
    table = jnp.full((HOLDERS, LANES), -1, jnp.int32).at[holder_ids, lane_of_edge].set(edge_ids, mode='drop')
    return (quanta, table)


def draw_quanta(key, part):
    return edge_tables(key)[0]


def draw_send_list(key, part):
    return edge_tables(key)[1]


def plant(drawn, own_key, smallest, largest):
    spot = [jax.random.randint(jax.random.fold_in(own_key, axis), (), 0, length) for axis, length in enumerate(drawn.shape)]
    main_axis = drawn.shape.index(max(drawn.shape))
    neighbour = spot[:main_axis] + [(spot[main_axis] + 1) % drawn.shape[main_axis]] + spot[main_axis + 1:]
    return drawn.at[tuple(spot)].set(smallest).at[tuple(neighbour)].set(largest)


def block_levels(rng, dims, cuts, smallest, largest):
    factor_of, own = 1.0, jax.random.fold_in(rng, 6)
    for axis_at, blocks in cuts:
        steps = jnp.exp(jax.random.uniform(jax.random.fold_in(own, axis_at), (blocks,), jnp.float32, smallest / len(cuts), largest / len(cuts)))
        factor_of = factor_of * jnp.repeat(steps, dims[axis_at] // blocks).reshape([-1 if axis == axis_at else 1 for axis in range(len(dims))])
    return factor_of


def noise(key, extent, width, reach, cuts=(), kind=jnp.bfloat16):
    values = width * jax.random.normal(key, extent, jnp.float32)
    if cuts:
        values = values * block_levels(key, extent, cuts, -0.22, 0.18)
    return jnp.clip(values, -reach, reach).astype(kind)


def setup_inputs(seed: int = 0) -> dict:
    arg_keys = jax.random.split(jax.random.key(seed), 10)
    section_state = noise(arg_keys[0], (AUX, 2 * SITES * SITES), 1.0, 6.0, ((0, 256),), jnp.float32)
    coupling = noise(arg_keys[1], (SITES, SITES), SITES ** -0.5, 0.625, (), jnp.float32)
    site_energy = jnp.clip(jax.random.uniform(arg_keys[2], (SITES,), jnp.float32, -1.0, 1.0), -1.0, 1.0)
    bath_rate = jnp.clip(jnp.exp(jax.random.uniform(arg_keys[3], (SITES,), jnp.float32, math.log(0.3), math.log(3.0))), 0.3, 3.0)
    bath_strength = jnp.clip(jnp.exp(jax.random.uniform(arg_keys[4], (SITES,), jnp.float32, math.log(0.1), math.log(1.0))), 0.1, 1.0)
    bath_of_site = jax.random.permutation(arg_keys[5], SITES).astype(jnp.int32)
    quanta = draw_quanta(jax.random.fold_in(arg_keys[9], 71), 0)
    send_list = draw_send_list(jax.random.fold_in(arg_keys[9], 71), 0)
    dest_slot = plant(jax.random.randint(arg_keys[8], (HOLDERS, LANES), 0, AUX_DEV), jax.random.fold_in(arg_keys[8], 1), 0, AUX_DEV - 1).astype(jnp.int32)
    return dict(section_state=section_state, coupling=coupling, site_energy=site_energy, bath_rate=bath_rate, bath_strength=bath_strength, bath_of_site=bath_of_site, quanta=quanta, send_list=send_list, dest_slot=dest_slot)


thermal = 0.5
highest = lax.Precision.HIGHEST


def local_block(hamilton, paired, holder_block, damp_block):
    site_count = hamilton.shape[0]
    left_product = jnp.einsum("ij,ajc->aic", hamilton, holder_block, precision=highest)
    right_product = jnp.dot(holder_block.reshape(-1, 2 * site_count), paired, precision=highest).reshape(holder_block.shape)
    commutator = left_product - right_product
    coherent = jnp.concatenate([commutator[..., site_count:], -commutator[..., :site_count]], axis=-1)
    return coherent - damp_block[:, None, None] * holder_block


def slice_pairs(states, holders, columns):
    site_count = states.shape[1]
    positions = jnp.arange(site_count).astype(jnp.int32)
    row_part = states[holders, columns, :]
    column_real = states[holders[:, None], positions[None, :], columns[:, None]]
    column_imag = states[holders[:, None], positions[None, :], columns[:, None] + site_count]
    return row_part, column_real, column_imag


def reference(section_state, coupling, site_energy, bath_rate, bath_strength, bath_of_site, quanta, send_list, dest_slot):
    float_type = section_state.dtype
    flat_shape = section_state.shape
    section_state = section_state.reshape(AUX, SITES, 2 * SITES)
    positions = jnp.arange(SITES).astype(jnp.int32)
    hamilton = (coupling + coupling.T) * 0.5 + jnp.diag(site_energy)
    zero_block = jnp.zeros_like(hamilton)
    paired = jnp.concatenate([jnp.concatenate([hamilton, zero_block], 1), jnp.concatenate([zero_block, hamilton], 1)], 0)
    chooser = (bath_of_site[:, None] == positions[None, :]).astype(float_type)
    site_rate = jnp.dot(chooser, bath_rate, precision=highest)
    site_strength = jnp.dot(chooser, bath_strength, precision=highest)
    real_coef = 2.0 * thermal * site_strength
    imag_coef = site_strength * site_rate
    matches = (quanta[:, :, None] == positions[None, None, :]).astype(float_type)
    multiple = jnp.sum(matches, axis=1)
    damping = jnp.dot(multiple, site_rate, precision=highest)
    blocks = section_state.reshape(HOLDERS, AUX_DEV, SITES, 2 * SITES)
    damp_blocks = damping.reshape(HOLDERS, AUX_DEV)
    derivative = lax.map(lambda pieces: local_block(hamilton, paired, pieces[0], pieces[1]), (blocks, damp_blocks)).reshape(section_state.shape)

    holder_ids = jnp.arange(HOLDERS).astype(jnp.int32)[:, None]
    lane_ids = jnp.arange(LANES).astype(jnp.int32)[None, :]
    band_ids = holder_ids // PEERS
    lane_group = lane_ids // (PEERS * CAP)
    target_peer = (lane_ids // CAP) % PEERS
    clipped = jnp.maximum(send_list, 0)
    sources = holder_ids * AUX_DEV + clipped // DEPTH
    lane_sites = quanta[sources, clipped % DEPTH]
    target_band = band_ids - lane_group
    usable = (send_list >= 0) & (lane_sites >= 0) & (target_band >= 0)
    targets = (jnp.maximum(target_band, 0) * PEERS + target_peer) * AUX_DEV + dest_slot
    sources = sources.reshape(-1).astype(jnp.int32)
    targets = targets.reshape(-1).astype(jnp.int32)
    columns = jnp.maximum(lane_sites, 0).reshape(-1).astype(jnp.int32)
    mask = usable.reshape(-1).astype(float_type)[:, None]

    upper_row, upper_creal, upper_cimag = slice_pairs(section_state, sources, columns)
    lower_row, lower_creal, lower_cimag = slice_pairs(section_state, targets, columns)

    up_row = jnp.concatenate([upper_row[:, SITES:], -upper_row[:, :SITES]], axis=-1)
    derivative = derivative.at[targets, columns, :].add(mask * up_row)
    derivative = derivative.at[targets[:, None], positions[None, :], columns[:, None]].add(mask * (-upper_cimag))
    derivative = derivative.at[targets[:, None], positions[None, :], columns[:, None] + SITES].add(mask * upper_creal)

    weights = multiple[sources, columns]
    shared = (-weights * imag_coef[columns])[:, None]
    row_turn = (-weights * real_coef[columns])[:, None]
    column_turn = (weights * real_coef[columns])[:, None]
    lower_rreal = lower_row[:, :SITES]
    lower_rimag = lower_row[:, SITES:]
    down_row = jnp.concatenate([shared * lower_rreal - row_turn * lower_rimag, shared * lower_rimag + row_turn * lower_rreal], axis=-1)
    down_creal = shared * lower_creal - column_turn * lower_cimag
    down_cimag = shared * lower_cimag + column_turn * lower_creal
    derivative = derivative.at[sources, columns, :].add(mask * down_row)
    derivative = derivative.at[sources[:, None], positions[None, :], columns[:, None]].add(mask * down_creal)
    derivative = derivative.at[sources[:, None], positions[None, :], columns[:, None] + SITES].add(mask * down_cimag)
    return derivative.reshape(flat_shape)
```

```python
import functools

import jax
import jax.numpy as jnp
from jax import lax
from jax.experimental import pallas as pl
from jax.experimental.pallas import tpu as pltpu
from jax.sharding import PartitionSpec as P

MESH = pl.DeviceIdType.MESH
F32 = jnp.float32
BF16 = jnp.bfloat16
SITES = 96
HALF = 48
SLOTS = 8
DEPTH = 4
PEERS = 32
TILES = 2 * PEERS
LANES = 128
TIERS = 8


def split_pair(value):
    high = value.astype(BF16)
    return high, (value - high.astype(F32)).astype(BF16)


def mxu(left, right):
    return jnp.dot(left, right, preferred_element_type=F32)


def permuted(site):
    return (site >> 1) + HALF * (site & 1)


def kernel(
    state_hbm,
    coupling_hbm,
    energy_hbm,
    rate_hbm,
    strength_hbm,
    bath_hbm,
    quanta_hbm,
    send_hbm,
    dest_hbm,
    result,
    raw,
    coupling_v,
    table_v,
    bath_v,
    quanta_v,
    send_v,
    dest_v,
    tag_out,
    tag_in,
    up_out,
    up_in,
    reply_out,
    reply_in,
    tag_cols,
    own_cols,
    rows_hi,
    rows_lo,
    cols_hi,
    cols_lo,
    total,
    load_sem,
    small_sem,
    send_sem,
    recv_sem,
):
    tier = lax.axis_index("tier")
    peer = lax.axis_index("aux")
    my_y = peer // 8
    my_x = lax.rem(peer, 8) // 2
    my_c = lax.rem(peer, 2)

    def far_first(step):
        def offset(k):
            return jnp.where(k == 0, 2, jnp.where(k == 1, 1, jnp.where(k == 2, 3, 0)))

        dy = offset(step // 8)
        dx = offset(lax.rem(step, 8) // 2)
        dc = 1 - lax.rem(step, 2)
        return lax.rem(my_y + dy, 4) * 8 + lax.rem(my_x + dx, 4) * 2 + lax.rem(my_c + dc, 2)

    barrier = pltpu.get_barrier_semaphore()

    @pl.when(tier < TIERS - 1)
    def _():
        def greet_above(step, carry):
            pl.semaphore_signal(
                barrier, inc=1, device_id=(tier + 1, far_first(step)), device_id_type=MESH
            )
            return carry

        lax.fori_loop(0, PEERS, greet_above, 0)

    def greet_band(step, carry):
        pl.semaphore_signal(
            barrier, inc=1, device_id=(tier, far_first(step)), device_id_type=MESH
        )
        return carry

    lax.fori_loop(0, PEERS - 1, greet_band, 0)

    small = [
        pltpu.make_async_copy(send_hbm, send_v, small_sem.at[0]),
        pltpu.make_async_copy(dest_hbm, dest_v, small_sem.at[1]),
        pltpu.make_async_copy(quanta_hbm, quanta_v, small_sem.at[2]),
        pltpu.make_async_copy(rate_hbm, table_v.at[0], small_sem.at[3]),
        pltpu.make_async_copy(strength_hbm, table_v.at[1], small_sem.at[4]),
        pltpu.make_async_copy(energy_hbm, table_v.at[2], small_sem.at[5]),
        pltpu.make_async_copy(bath_hbm, bath_v, small_sem.at[6]),
        pltpu.make_async_copy(coupling_hbm, coupling_v, small_sem.at[7]),
    ]
    for copy in small:
        copy.start()
    load = pltpu.make_async_copy(state_hbm, raw, load_sem)
    load.start()
    for copy in small:
        copy.wait()

    lane = lax.broadcasted_iota(jnp.int32, (1, LANES), 1)
    sub8 = lax.broadcasted_iota(jnp.int32, (SLOTS, LANES), 0)
    sub96 = lax.broadcasted_iota(jnp.int32, (SITES, LANES), 0)
    quanta = jnp.concatenate(
        [
            jnp.concatenate([quanta_v[...], jnp.zeros((DEPTH, LANES - SLOTS), jnp.int32)], axis=1),
            jnp.zeros((SLOTS - DEPTH, LANES), jnp.int32),
        ],
        axis=0,
    ).T[:SLOTS]

    def quanta_of(entry):
        slot = entry >> 2
        place = entry & 3
        hit = sub8 == jnp.broadcast_to(slot, (SLOTS, LANES))
        found = [
            jnp.sum(
                jnp.where(hit, jnp.broadcast_to(quanta[:, p : p + 1], (SLOTS, LANES)), 0),
                axis=0,
                keepdims=True,
            )
            for p in range(DEPTH)
        ]
        site = found[3]
        for p in range(DEPTH - 1):
            site = jnp.where(place == p, found[p], site)
        count = sum((found[p] == site).astype(F32) for p in range(DEPTH))
        return slot, site, count

    pad = jnp.zeros((1, LANES - SITES), F32)
    base = jnp.concatenate(
        [
            jnp.concatenate([bath_v[...].astype(F32), pad], axis=1),
            jnp.concatenate([table_v[0], pad], axis=1),
            jnp.concatenate([table_v[1], pad], axis=1),
            jnp.concatenate([table_v[2], pad], axis=1),
            jnp.zeros((LANES - 4, LANES), F32),
        ],
        axis=0,
    ).T
    bath_col = base[:SITES, 0:1]
    rate_col = base[:SITES, 1:2]
    strength_col = base[:SITES, 2:3]
    sub96f = sub96.astype(F32)

    def look_up(site, columns):
        hit = sub96 == jnp.broadcast_to(site, (SITES, LANES))
        bath = jnp.sum(
            jnp.where(hit, jnp.broadcast_to(bath_col, (SITES, LANES)), 0.0), axis=0, keepdims=True
        )
        hit = sub96f == jnp.broadcast_to(bath, (SITES, LANES))
        return [
            jnp.sum(
                jnp.where(hit, jnp.broadcast_to(column, (SITES, LANES)), 0.0), axis=0, keepdims=True
            )
            for column in columns
        ]

    entry = send_v[...]
    slot, site, weight = quanta_of(jnp.maximum(entry, 0))
    group = lane // (LANES // 2)
    usable = (entry >= 0) & (site >= 0) & (tier - group >= 0)
    strength_l, rate_l = look_up(site, [strength_col, rate_col])
    lower = dest_v[...]

    def marked(value):
        return jnp.where(usable, value, -1).astype(F32)

    tags = jnp.concatenate(
        [
            marked(slot * LANES + permuted(site)),
            marked(slot * LANES + site),
            marked(lower * LANES + permuted(site)),
            marked(lower * LANES + site),
            jnp.where(usable, -weight * (strength_l * rate_l), 0.0),
            jnp.where(usable, weight * strength_l, 0.0),
            jnp.zeros((LANES - 6, LANES), F32),
        ],
        axis=0,
    ).T
    tag_cols[...] = tags
    for c in range(2):
        half = tag_cols[pl.ds(c, TILES, stride=2), :]
        own_cols[c * TILES : (c + 1) * TILES, :] = half
        tag_out[pl.ds(c, TILES, stride=8), :] = half
    tag_tiles = tag_out.reshape(TILES, 8, LANES)
    tag_in_tiles = tag_in.reshape(TILES, 8, LANES)
    up_tiles = up_out.reshape(TILES, 8, LANES)
    up_in_tiles = up_in.reshape(TILES, 8, LANES)
    reply_tiles = reply_out.reshape(TILES, 8, LANES)
    reply_in_tiles = reply_in.reshape(TILES, 8, LANES)

    def exchange(source, target, rows, which, step_tier, allowed):
        other = tier + step_tier

        @pl.when(allowed)
        def _():
            def far(step, carry):
                q = far_first(step)
                pltpu.make_async_remote_copy(
                    source.at[PEERS + q, pl.ds(0, rows)],
                    target.at[PEERS + peer, pl.ds(0, rows)],
                    send_sem.at[which],
                    recv_sem.at[2 * which + 1],
                    device_id=(other, q),
                    device_id_type=MESH,
                ).start()
                return carry

            lax.fori_loop(0, PEERS, far, 0)

        def near(step, carry):
            q = far_first(step)
            pltpu.make_async_remote_copy(
                source.at[q, pl.ds(0, rows)],
                target.at[peer, pl.ds(0, rows)],
                send_sem.at[which],
                recv_sem.at[2 * which],
                device_id=(tier, q),
                device_id_type=MESH,
            ).start()
            return carry

        lax.fori_loop(0, PEERS - 1, near, 0)

    def await_all(target, rows, which, near_sem, far_sem, far_allowed):
        block = target.at[pl.ds(0, PEERS - 1), pl.ds(0, rows)]
        pltpu.make_async_copy(block, block, near_sem).wait()

        @pl.when(far_allowed)
        def _():
            block = target.at[pl.ds(0, PEERS), pl.ds(0, rows)]
            pltpu.make_async_copy(block, block, far_sem).wait()

    def received(target, rows, which, far_allowed):
        await_all(target, rows, which, recv_sem.at[2 * which], recv_sem.at[2 * which + 1], far_allowed)

    def sent(target, rows, which, far_allowed):
        await_all(target, rows, which, send_sem.at[which], send_sem.at[which], far_allowed)

    has_lower = tier > 0
    has_upper = tier < TIERS - 1

    self_row = pl.multiple_of(peer * 8, 8)
    tag_in[pl.ds(self_row, 8), :] = tag_out[pl.ds(self_row, 8), :]

    @pl.when(tier == TIERS - 1)
    def _():
        tag_in[PEERS * 8 :, :] = jnp.full((PEERS * 8, LANES), -1.0, F32)
        up_in[PEERS * 8 :, :] = jnp.zeros((PEERS * 8, LANES), F32)

    @pl.when(tier == 0)
    def _():
        reply_in[PEERS * 8 :, :] = jnp.zeros((PEERS * 8, LANES), F32)

    pl.semaphore_wait(barrier, jnp.where(has_lower, 2 * PEERS - 1, PEERS - 1))

    exchange(tag_tiles, tag_in_tiles, 2, 0, -1, has_lower)

    load.wait()
    lane48 = lax.broadcasted_iota(jnp.int32, (HALF, LANES), 1)
    zero48 = jnp.zeros((HALF, LANES), F32)
    for a in range(SLOTS):
        t0 = raw[pl.ds(a, HALF, stride=24), :]
        t1 = raw[pl.ds(8 + a, HALF, stride=24), :]
        t2 = raw[pl.ds(16 + a, HALF, stride=24), :]
        ok = lane48 < SITES
        even_re = jnp.where(ok, t0, zero48)
        even_im = jnp.where(
            lane48 < 32, pltpu.roll(t0, 32, 1), jnp.where(ok, pltpu.roll(t1, 32, 1), zero48)
        )
        odd_re = jnp.where(
            lane48 < 64, pltpu.roll(t1, 64, 1), jnp.where(ok, pltpu.roll(t2, 64, 1), zero48)
        )
        odd_im = jnp.where(ok, pltpu.roll(t2, 96, 1), zero48)
        gap = jnp.zeros((LANES - SITES, LANES), F32)
        real = jnp.concatenate([even_re, odd_re, gap], axis=0)
        imag = jnp.concatenate([even_im, odd_im, gap], axis=0)
        both = jnp.concatenate([real, imag], axis=1)
        high, low = split_pair(both)
        block = slice(a * LANES, (a + 1) * LANES)
        rows_hi[block, :] = high
        rows_lo[block, :] = low
        turned = jnp.concatenate([real.T, imag.T], axis=1)
        high, low = split_pair(turned)
        cols_hi[block, :] = high
        cols_lo[block, :] = low

    lane1024 = lax.broadcasted_iota(jnp.int32, (LANES, SLOTS * LANES), 1).astype(F32)

    def one_hot(column):
        return jnp.where(
            lane1024 == jnp.broadcast_to(column, (LANES, SLOTS * LANES)), 1.0, 0.0
        ).astype(BF16)

    def gather(row_hot, col_hot):
        rows = mxu(row_hot, rows_hi[...]) + mxu(row_hot, rows_lo[...])
        cols = mxu(col_hot, cols_hi[...]) + mxu(col_hot, cols_lo[...])
        return rows, cols

    def put_tiles(target, rows, cols):
        for c in range(2):
            lanes = slice(c * TILES, (c + 1) * TILES)
            target[pl.ds(4 * c, TILES, stride=8), :] = rows[lanes, :LANES]
            target[pl.ds(4 * c + 1, TILES, stride=8), :] = rows[lanes, LANES:]
            target[pl.ds(4 * c + 2, TILES, stride=8), :] = cols[lanes, :LANES]
            target[pl.ds(4 * c + 3, TILES, stride=8), :] = cols[lanes, LANES:]

    def get_tiles(source):
        def piece(k):
            return jnp.concatenate(
                [source[pl.ds(4 * c + k, TILES, stride=8), :] for c in range(2)], axis=0
            )

        return piece(0), piece(1), piece(2), piece(3)

    own = own_cols[...]
    own_col_hot = one_hot(own[:, 1:2])
    rows, cols = gather(one_hot(own[:, 0:1]), own_col_hot)
    put_tiles(up_out, rows, cols)
    up_in[pl.ds(self_row, 8), :] = up_out[pl.ds(self_row, 8), :]
    exchange(up_tiles, up_in_tiles, 8, 1, -1, has_lower)

    received(tag_in_tiles, 2, 0, has_upper)
    asked = jnp.concatenate([tag_in[pl.ds(c, TILES, stride=8), :] for c in range(2)], axis=0)
    asked_col_hot = one_hot(asked[:, 3:4])
    rows, cols = gather(one_hot(asked[:, 2:3]), asked_col_hot)
    put_tiles(reply_out, rows, cols)
    exchange(reply_tiles, reply_in_tiles, 8, 2, 1, has_upper)
    reply_in[pl.ds(self_row, 8), :] = reply_out[pl.ds(self_row, 8), :]

    diagonal = lax.broadcasted_iota(jnp.int32, (SITES, SITES), 0) == lax.broadcasted_iota(
        jnp.int32, (SITES, SITES), 1
    )
    coupling = coupling_v[...]
    hamilton = (coupling + coupling.T) * 0.5 + jnp.where(
        diagonal, jnp.broadcast_to(base[:SITES, 3:4], (SITES, SITES)), 0.0
    )
    row_id = lax.broadcasted_iota(jnp.int32, (SITES, SITES), 0)
    natural = jnp.where(row_id < HALF, 2 * row_id, 2 * (row_id - HALF) + 1)
    chooser = jnp.where(
        natural == lax.broadcasted_iota(jnp.int32, (SITES, SITES), 1), 1.0, 0.0
    ).astype(BF16)
    h_hi, h_lo = split_pair(hamilton)
    p_hi = mxu(chooser, h_hi).astype(BF16)
    p_lo = mxu(chooser, h_lo).astype(BF16)
    p_hi = mxu(p_hi, chooser.T).astype(BF16)
    p_lo = mxu(p_lo, chooser.T).astype(BF16)
    gap_r = jnp.zeros((SITES, LANES - SITES), BF16)
    left_hi = jnp.concatenate([p_hi, gap_r], axis=1)
    left_lo = jnp.concatenate([p_lo, gap_r], axis=1)
    gap_b = jnp.zeros((LANES - SITES, LANES), BF16)

    def turned_pair(h):
        square = jnp.concatenate([jnp.concatenate([h, gap_r], axis=1), gap_b], axis=0)
        empty = jnp.zeros((LANES, LANES), BF16)
        return jnp.concatenate(
            [
                jnp.concatenate([empty, square], axis=1),
                jnp.concatenate([-square, empty], axis=1),
            ],
            axis=0,
        )

    right_hi = turned_pair(h_hi)
    right_lo = turned_pair(h_lo)

    edge_slot, edge_site, _ = quanta_of(jnp.minimum(lane, SLOTS * DEPTH - 1))
    (edge_rate,) = look_up(edge_site, [rate_col])
    edge_rate = jnp.where((lane < SLOTS * DEPTH) & (edge_site >= 0), edge_rate, 0.0)
    damping = jnp.sum(
        jnp.where(
            sub8 == jnp.broadcast_to(edge_slot, (SLOTS, LANES)),
            jnp.broadcast_to(edge_rate, (SLOTS, LANES)),
            0.0,
        ),
        axis=1,
        keepdims=True,
    )

    for a in range(SLOTS):
        z_hi = rows_hi[a * LANES : (a + 1) * LANES, :]
        z_lo = rows_lo[a * LANES : (a + 1) * LANES, :]
        left = mxu(left_hi, z_hi) + mxu(left_hi, z_lo) + mxu(left_lo, z_hi)
        z_hi = z_hi[:SITES]
        z_lo = z_lo[:SITES]
        right = mxu(z_hi, right_hi) + mxu(z_lo, right_hi) + mxu(z_hi, right_lo)
        z = z_hi.astype(F32) + z_lo.astype(F32)
        total[a * SITES : (a + 1) * SITES, :] = (
            jnp.concatenate([left[:, LANES:], -left[:, :LANES]], axis=1)
            + right
            - damping[a : a + 1, 0:1] * z
        )

    sub768 = lax.broadcasted_iota(jnp.int32, (SLOTS, SITES, LANES), 1) + LANES * (
        lax.broadcasted_iota(jnp.int32, (SLOTS, SITES, LANES), 0)
    )
    sub768 = sub768.astype(F32).reshape(SLOTS * SITES, LANES)

    def scatter_hots(columns, which, col_hot):
        row = columns.T[which : which + 1, :]
        hot = jnp.where(
            sub768 == jnp.broadcast_to(row, (SLOTS * SITES, LANES)), 1.0, 0.0
        ).astype(BF16)
        return jnp.concatenate([hot, hot], axis=1), jnp.concatenate([col_hot, col_hot], axis=0)

    def scatter(row_hots, col_hots, row_data, col_re, col_im):
        high, low = split_pair(row_data)
        by_row = mxu(row_hots, jnp.concatenate([high, low], axis=0))
        turned = jnp.concatenate([col_re.T[:SITES], col_im.T[:SITES]], axis=0)
        high, low = split_pair(turned)
        by_col = mxu(jnp.concatenate([high, low], axis=1), col_hots)
        return by_row, by_col

    def block_of(parts, a):
        by_row, by_col = parts
        lanes = slice(a * LANES, (a + 1) * LANES)
        return by_row[a * SITES : (a + 1) * SITES] + jnp.concatenate(
            [by_col[:SITES, lanes], by_col[SITES:, lanes]], axis=1
        )

    asked_hots = scatter_hots(asked, 2, asked_col_hot)
    own_hots = scatter_hots(own, 0, own_col_hot)
    received(up_in_tiles, 8, 1, has_upper)
    row_re, row_im, col_re, col_im = get_tiles(up_in)
    parts = scatter(*asked_hots, jnp.concatenate([row_im, -row_re], axis=1), -col_im, col_re)
    for a in range(SLOTS):
        total[a * SITES : (a + 1) * SITES, :] += block_of(parts, a)

    received(reply_in_tiles, 8, 2, has_lower)
    row_re, row_im, col_re, col_im = get_tiles(reply_in)
    shared = jnp.broadcast_to(own[:, 4:5], (LANES, LANES))
    turn = jnp.broadcast_to(own[:, 5:6], (LANES, LANES))
    parts = scatter(
        *own_hots,
        jnp.concatenate([shared * row_re + turn * row_im, shared * row_im - turn * row_re], axis=1),
        shared * col_re - turn * col_im,
        shared * col_im + turn * col_re,
    )
    for a in range(SLOTS):
        value = total[a * SITES : (a + 1) * SITES, :] + block_of(parts, a)
        even_re, odd_re = value[:HALF, :LANES], value[HALF:, :LANES]
        even_im, odd_im = value[:HALF, LANES:], value[HALF:, LANES:]
        even_im = pltpu.roll(even_im, 96, 1)
        odd_re = pltpu.roll(odd_re, 64, 1)
        odd_im = pltpu.roll(odd_im, 32, 1)
        result[pl.ds(a, HALF, stride=24), :] = jnp.where(lane48 < SITES, even_re, even_im)
        result[pl.ds(8 + a, HALF, stride=24), :] = jnp.where(lane48 < 64, even_im, odd_re)
        result[pl.ds(16 + a, HALF, stride=24), :] = jnp.where(lane48 < 32, odd_re, odd_im)
    sent(tag_in_tiles, 2, 0, has_lower)
    sent(up_in_tiles, 8, 1, has_lower)
    sent(reply_in_tiles, 8, 2, has_upper)


def on_device(
    section_state,
    coupling,
    site_energy,
    bath_rate,
    bath_strength,
    bath_of_site,
    quanta,
    send_list,
    dest_slot,
):
    slots, width = section_state.shape
    chunks = width // LANES
    tiled = section_state.reshape(slots, chunks, LANES).transpose(1, 0, 2).reshape(-1, LANES)
    operands = (
        tiled,
        coupling,
        site_energy.reshape(1, SITES),
        bath_rate.reshape(1, SITES),
        bath_strength.reshape(1, SITES),
        bath_of_site.reshape(1, SITES),
        quanta.T,
        send_list,
        dest_slot,
    )
    tile_buffer = pltpu.VMEM((TILES * 8, LANES), F32)
    out = pl.pallas_call(
        kernel,
        out_shape=pltpu.VMEM(tiled.shape, F32),
        in_specs=[pl.BlockSpec(memory_space=pltpu.HBM)] * 9,
        out_specs=pl.BlockSpec(memory_space=pltpu.VMEM),
        scratch_shapes=[
            pltpu.VMEM(tiled.shape, F32),
            pltpu.VMEM((SITES, SITES), F32),
            pltpu.VMEM((3, 1, SITES), F32),
            pltpu.VMEM((1, SITES), jnp.int32),
            pltpu.VMEM((DEPTH, SLOTS), jnp.int32),
            pltpu.VMEM((1, LANES), jnp.int32),
            pltpu.VMEM((1, LANES), jnp.int32),
            tile_buffer,
            tile_buffer,
            tile_buffer,
            tile_buffer,
            tile_buffer,
            tile_buffer,
            pltpu.VMEM((LANES, LANES), F32),
            pltpu.VMEM((LANES, LANES), F32),
            pltpu.VMEM((SLOTS * LANES, 2 * LANES), BF16),
            pltpu.VMEM((SLOTS * LANES, 2 * LANES), BF16),
            pltpu.VMEM((SLOTS * LANES, 2 * LANES), BF16),
            pltpu.VMEM((SLOTS * LANES, 2 * LANES), BF16),
            pltpu.VMEM((SLOTS * SITES, 2 * LANES), F32),
            pltpu.SemaphoreType.DMA,
            pltpu.SemaphoreType.DMA((8,)),
            pltpu.SemaphoreType.DMA((3,)),
            pltpu.SemaphoreType.DMA((6,)),
        ],
        compiler_params=pltpu.CompilerParams(
            collective_id=0, has_side_effects=True, vmem_limit_bytes=32 * 1024 * 1024
        ),
    )(*[pltpu.with_memory_space_constraint(value, pltpu.HBM) for value in operands])
    return out.reshape(chunks, slots, LANES).transpose(1, 0, 2).reshape(slots, width)


def solution(mesh):
    return jax.shard_map(
        on_device,
        mesh=mesh,
        in_specs=(
            P(("tier", "aux"), None),
            P(),
            P(),
            P(),
            P(),
            P(),
            P(("tier", "aux"), None),
            P(("tier", "aux"), None),
            P(("tier", "aux"), None),
        ),
        out_specs=P(("tier", "aux"), None),
        check_vma=False,
    )
```

```python
import functools

import jax
import jax.numpy as jnp
from jax import lax
from jax.experimental import pallas as pl
from jax.experimental.pallas import tpu as pltpu
from jax.sharding import PartitionSpec as P

MESH = pl.DeviceIdType.MESH
F32 = jnp.float32
BF16 = jnp.bfloat16
SITES = 96
HALF = 48
SLOTS = 8
DEPTH = 4
PEERS = 32
TILES = 2 * PEERS
LANES = 128
TIERS = 8


def routes():
    found = [
        (across, dy, dx, dc)
        for across in range(2)
        for dy in range(4)
        for dx in range(4)
        for dc in range(2)
        if (across, dy, dx, dc) != (0, 0, 0, 0)
    ]
    return sorted(found, key=lambda s: (-(s[0] + min(s[1], 4 - s[1]) + min(s[2], 4 - s[2])), -s[3]))


ROUTES = routes()


def split_pair(value):
    high = value.astype(BF16)
    return high, (value - high.astype(F32)).astype(BF16)


def mxu(left, right):
    return jnp.dot(left, right, preferred_element_type=F32)


def permuted(site):
    return (site >> 1) + HALF * (site & 1)


def kernel(
    state_hbm,
    coupling_hbm,
    energy_hbm,
    rate_hbm,
    strength_hbm,
    bath_hbm,
    quanta_hbm,
    send_hbm,
    dest_hbm,
    result,
    raw,
    coupling_v,
    table_v,
    bath_v,
    quanta_v,
    send_v,
    dest_v,
    tag_out,
    tag_in,
    up_out,
    up_in,
    reply_out,
    reply_in,
    tag_cols,
    own_cols,
    rows_hi,
    rows_lo,
    cols_hi,
    cols_lo,
    total,
    load_sem,
    small_sem,
    send_sem,
    recv_sem,
):
    tier = lax.axis_index("tier")
    peer = lax.axis_index("aux")
    my_y = peer // 8
    my_x = lax.rem(peer, 8) // 2
    my_c = lax.rem(peer, 2)

    def partner(dy, dx, dc):
        return lax.rem(my_y + dy, 4) * 8 + lax.rem(my_x + dx, 4) * 2 + lax.rem(my_c + dc, 2)

    barrier = pltpu.get_barrier_semaphore()

    def greet(up, dy, dx, dc):
        pl.semaphore_signal(
            barrier,
            inc=1,
            device_id=(tier + up, partner(dy, dx, dc)),
            device_id_type=MESH,
        )

    def farthest_first(act, allowed):
        @pl.when(allowed)
        def _():
            for hop in ROUTES:
                act(*hop)

        @pl.when(jnp.logical_not(allowed))
        def _():
            for hop in ROUTES:
                if not hop[0]:
                    act(*hop)

    has_lower = tier > 0
    has_upper = tier < TIERS - 1
    farthest_first(greet, has_upper)

    small = [
        pltpu.make_async_copy(send_hbm, send_v, small_sem.at[0]),
        pltpu.make_async_copy(dest_hbm, dest_v, small_sem.at[1]),
        pltpu.make_async_copy(quanta_hbm, quanta_v, small_sem.at[2]),
        pltpu.make_async_copy(rate_hbm, table_v.at[0], small_sem.at[3]),
        pltpu.make_async_copy(strength_hbm, table_v.at[1], small_sem.at[4]),
        pltpu.make_async_copy(energy_hbm, table_v.at[2], small_sem.at[5]),
        pltpu.make_async_copy(bath_hbm, bath_v, small_sem.at[6]),
        pltpu.make_async_copy(coupling_hbm, coupling_v, small_sem.at[7]),
    ]
    for copy in small:
        copy.start()
    load = pltpu.make_async_copy(state_hbm, raw, load_sem)
    load.start()
    for copy in small:
        copy.wait()

    lane = lax.broadcasted_iota(jnp.int32, (1, LANES), 1)
    sub8 = lax.broadcasted_iota(jnp.int32, (SLOTS, LANES), 0)
    sub96 = lax.broadcasted_iota(jnp.int32, (SITES, LANES), 0)
    quanta = jnp.concatenate(
        [
            jnp.concatenate([quanta_v[...], jnp.zeros((DEPTH, LANES - SLOTS), jnp.int32)], axis=1),
            jnp.zeros((SLOTS - DEPTH, LANES), jnp.int32),
        ],
        axis=0,
    ).T[:SLOTS]

    def quanta_of(entry):
        slot = entry >> 2
        place = entry & 3
        hit = sub8 == jnp.broadcast_to(slot, (SLOTS, LANES))
        found = [
            jnp.sum(
                jnp.where(hit, jnp.broadcast_to(quanta[:, p : p + 1], (SLOTS, LANES)), 0),
                axis=0,
                keepdims=True,
            )
            for p in range(DEPTH)
        ]
        site = found[3]
        for p in range(DEPTH - 1):
            site = jnp.where(place == p, found[p], site)
        count = sum((found[p] == site).astype(F32) for p in range(DEPTH))
        return slot, site, count

    pad = jnp.zeros((1, LANES - SITES), F32)
    base = jnp.concatenate(
        [
            jnp.concatenate([bath_v[...].astype(F32), pad], axis=1),
            jnp.concatenate([table_v[0], pad], axis=1),
            jnp.concatenate([table_v[1], pad], axis=1),
            jnp.concatenate([table_v[2], pad], axis=1),
            jnp.zeros((LANES - 4, LANES), F32),
        ],
        axis=0,
    ).T
    bath_col = base[:SITES, 0:1]
    rate_col = base[:SITES, 1:2]
    strength_col = base[:SITES, 2:3]
    sub96f = sub96.astype(F32)

    def look_up(site, columns):
        hit = sub96 == jnp.broadcast_to(site, (SITES, LANES))
        bath = jnp.sum(
            jnp.where(hit, jnp.broadcast_to(bath_col, (SITES, LANES)), 0.0), axis=0, keepdims=True
        )
        hit = sub96f == jnp.broadcast_to(bath, (SITES, LANES))
        return [
            jnp.sum(
                jnp.where(hit, jnp.broadcast_to(column, (SITES, LANES)), 0.0), axis=0, keepdims=True
            )
            for column in columns
        ]

    entry = send_v[...]
    slot, site, weight = quanta_of(jnp.maximum(entry, 0))
    group = lane // (LANES // 2)
    usable = (entry >= 0) & (site >= 0) & (tier - group >= 0)
    strength_l, rate_l = look_up(site, [strength_col, rate_col])
    lower = dest_v[...]

    def marked(value):
        return jnp.where(usable, value, -1).astype(F32)

    tags = jnp.concatenate(
        [
            marked(slot * LANES + permuted(site)),
            marked(slot * LANES + site),
            marked(lower * LANES + permuted(site)),
            marked(lower * LANES + site),
            jnp.where(usable, -weight * (strength_l * rate_l), 0.0),
            jnp.where(usable, weight * strength_l, 0.0),
            jnp.zeros((LANES - 6, LANES), F32),
        ],
        axis=0,
    ).T
    tag_cols[...] = tags
    for c in range(2):
        half = tag_cols[pl.ds(c, TILES, stride=2), :]
        own_cols[c * TILES : (c + 1) * TILES, :] = half
        tag_out[pl.ds(c, TILES, stride=8), :] = half
    tag_tiles = tag_out.reshape(TILES, 8, LANES)
    tag_in_tiles = tag_in.reshape(TILES, 8, LANES)
    up_tiles = up_out.reshape(TILES, 8, LANES)
    up_in_tiles = up_in.reshape(TILES, 8, LANES)
    reply_tiles = reply_out.reshape(TILES, 8, LANES)
    reply_in_tiles = reply_in.reshape(TILES, 8, LANES)

    def exchange(source, target, rows, which, step_tier, allowed):
        def send(across, dy, dx, dc):
            q = partner(dy, dx, dc)
            pltpu.make_async_remote_copy(
                source.at[PEERS * across + q, pl.ds(0, rows)],
                target.at[PEERS * across + peer, pl.ds(0, rows)],
                send_sem.at[which],
                recv_sem.at[2 * which + across],
                device_id=(tier + step_tier * across, q),
                device_id_type=MESH,
            ).start()

        farthest_first(send, allowed)

    def await_all(target, rows, which, near_sem, far_sem, far_allowed):
        block = target.at[pl.ds(0, PEERS - 1), pl.ds(0, rows)]
        pltpu.make_async_copy(block, block, near_sem).wait()

        @pl.when(far_allowed)
        def _():
            block = target.at[pl.ds(0, PEERS), pl.ds(0, rows)]
            pltpu.make_async_copy(block, block, far_sem).wait()

    def received(target, rows, which, far_allowed):
        await_all(target, rows, which, recv_sem.at[2 * which], recv_sem.at[2 * which + 1], far_allowed)

    def sent(target, rows, which, far_allowed):
        await_all(target, rows, which, send_sem.at[which], send_sem.at[which], far_allowed)

    self_row = pl.multiple_of(peer * 8, 8)
    tag_in[pl.ds(self_row, 8), :] = tag_out[pl.ds(self_row, 8), :]

    @pl.when(tier == TIERS - 1)
    def _():
        tag_in[PEERS * 8 :, :] = jnp.full((PEERS * 8, LANES), -1.0, F32)
        up_in[PEERS * 8 :, :] = jnp.zeros((PEERS * 8, LANES), F32)

    @pl.when(tier == 0)
    def _():
        reply_in[PEERS * 8 :, :] = jnp.zeros((PEERS * 8, LANES), F32)

    pl.semaphore_wait(barrier, jnp.where(has_lower, 2 * PEERS - 1, PEERS - 1))

    exchange(tag_tiles, tag_in_tiles, 2, 0, -1, has_lower)

    load.wait()
    lane48 = lax.broadcasted_iota(jnp.int32, (HALF, LANES), 1)
    zero48 = jnp.zeros((HALF, LANES), F32)
    for a in range(SLOTS):
        t0 = raw[pl.ds(a, HALF, stride=24), :]
        t1 = raw[pl.ds(8 + a, HALF, stride=24), :]
        t2 = raw[pl.ds(16 + a, HALF, stride=24), :]
        ok = lane48 < SITES
        even_re = jnp.where(ok, t0, zero48)
        even_im = jnp.where(
            lane48 < 32, pltpu.roll(t0, 32, 1), jnp.where(ok, pltpu.roll(t1, 32, 1), zero48)
        )
        odd_re = jnp.where(
            lane48 < 64, pltpu.roll(t1, 64, 1), jnp.where(ok, pltpu.roll(t2, 64, 1), zero48)
        )
        odd_im = jnp.where(ok, pltpu.roll(t2, 96, 1), zero48)
        gap = jnp.zeros((LANES - SITES, LANES), F32)
        real = jnp.concatenate([even_re, odd_re, gap], axis=0)
        imag = jnp.concatenate([even_im, odd_im, gap], axis=0)
        both = jnp.concatenate([real, imag], axis=1)
        high, low = split_pair(both)
        block = slice(a * LANES, (a + 1) * LANES)
        rows_hi[block, :] = high
        rows_lo[block, :] = low
        turned = jnp.concatenate([real.T, imag.T], axis=1)
        high, low = split_pair(turned)
        cols_hi[block, :] = high
        cols_lo[block, :] = low

    lane1024 = lax.broadcasted_iota(jnp.int32, (LANES, SLOTS * LANES), 1).astype(F32)

    def one_hot(column):
        return jnp.where(
            lane1024 == jnp.broadcast_to(column, (LANES, SLOTS * LANES)), 1.0, 0.0
        ).astype(BF16)

    def gather(row_hot, col_hot):
        rows = mxu(row_hot, rows_hi[...]) + mxu(row_hot, rows_lo[...])
        cols = mxu(col_hot, cols_hi[...]) + mxu(col_hot, cols_lo[...])
        return rows, cols

    def put_tiles(target, rows, cols):
        for c in range(2):
            lanes = slice(c * TILES, (c + 1) * TILES)
            target[pl.ds(4 * c, TILES, stride=8), :] = rows[lanes, :LANES]
            target[pl.ds(4 * c + 1, TILES, stride=8), :] = rows[lanes, LANES:]
            target[pl.ds(4 * c + 2, TILES, stride=8), :] = cols[lanes, :LANES]
            target[pl.ds(4 * c + 3, TILES, stride=8), :] = cols[lanes, LANES:]

    def get_tiles(source):
        def piece(k):
            return jnp.concatenate(
                [source[pl.ds(4 * c + k, TILES, stride=8), :] for c in range(2)], axis=0
            )

        return piece(0), piece(1), piece(2), piece(3)

    own = own_cols[...]
    own_col_hot = one_hot(own[:, 1:2])
    rows, cols = gather(one_hot(own[:, 0:1]), own_col_hot)
    put_tiles(up_out, rows, cols)
    up_in[pl.ds(self_row, 8), :] = up_out[pl.ds(self_row, 8), :]
    exchange(up_tiles, up_in_tiles, 8, 1, -1, has_lower)

    received(tag_in_tiles, 2, 0, has_upper)
    asked = jnp.concatenate([tag_in[pl.ds(c, TILES, stride=8), :] for c in range(2)], axis=0)
    asked_col_hot = one_hot(asked[:, 3:4])
    rows, cols = gather(one_hot(asked[:, 2:3]), asked_col_hot)
    put_tiles(reply_out, rows, cols)
    exchange(reply_tiles, reply_in_tiles, 8, 2, 1, has_upper)
    reply_in[pl.ds(self_row, 8), :] = reply_out[pl.ds(self_row, 8), :]

    diagonal = lax.broadcasted_iota(jnp.int32, (SITES, SITES), 0) == lax.broadcasted_iota(
        jnp.int32, (SITES, SITES), 1
    )
    coupling = coupling_v[...]
    hamilton = (coupling + coupling.T) * 0.5 + jnp.where(
        diagonal, jnp.broadcast_to(base[:SITES, 3:4], (SITES, SITES)), 0.0
    )
    row_id = lax.broadcasted_iota(jnp.int32, (SITES, SITES), 0)
    natural = jnp.where(row_id < HALF, 2 * row_id, 2 * (row_id - HALF) + 1)
    chooser = jnp.where(
        natural == lax.broadcasted_iota(jnp.int32, (SITES, SITES), 1), 1.0, 0.0
    ).astype(BF16)
    h_hi, h_lo = split_pair(hamilton)
    p_hi = mxu(chooser, h_hi).astype(BF16)
    p_lo = mxu(chooser, h_lo).astype(BF16)
    p_hi = mxu(p_hi, chooser.T).astype(BF16)
    p_lo = mxu(p_lo, chooser.T).astype(BF16)
    gap_r = jnp.zeros((SITES, LANES - SITES), BF16)
    left_hi = jnp.concatenate([p_hi, gap_r], axis=1)
    left_lo = jnp.concatenate([p_lo, gap_r], axis=1)
    gap_b = jnp.zeros((LANES - SITES, LANES), BF16)

    def turned_pair(h):
        square = jnp.concatenate([jnp.concatenate([h, gap_r], axis=1), gap_b], axis=0)
        empty = jnp.zeros((LANES, LANES), BF16)
        return jnp.concatenate(
            [
                jnp.concatenate([empty, square], axis=1),
                jnp.concatenate([-square, empty], axis=1),
            ],
            axis=0,
        )

    right_hi = turned_pair(h_hi)
    right_lo = turned_pair(h_lo)

    edge_slot, edge_site, _ = quanta_of(jnp.minimum(lane, SLOTS * DEPTH - 1))
    (edge_rate,) = look_up(edge_site, [rate_col])
    edge_rate = jnp.where((lane < SLOTS * DEPTH) & (edge_site >= 0), edge_rate, 0.0)
    damping = jnp.sum(
        jnp.where(
            sub8 == jnp.broadcast_to(edge_slot, (SLOTS, LANES)),
            jnp.broadcast_to(edge_rate, (SLOTS, LANES)),
            0.0,
        ),
        axis=1,
        keepdims=True,
    )

    for a in range(SLOTS):
        z_hi = rows_hi[a * LANES : (a + 1) * LANES, :]
        z_lo = rows_lo[a * LANES : (a + 1) * LANES, :]
        left = mxu(left_hi, z_hi) + mxu(left_hi, z_lo) + mxu(left_lo, z_hi)
        z_hi = z_hi[:SITES]
        z_lo = z_lo[:SITES]
        right = mxu(z_hi, right_hi) + mxu(z_lo, right_hi) + mxu(z_hi, right_lo)
        z = z_hi.astype(F32) + z_lo.astype(F32)
        total[a * SITES : (a + 1) * SITES, :] = (
            jnp.concatenate([left[:, LANES:], -left[:, :LANES]], axis=1)
            + right
            - damping[a : a + 1, 0:1] * z
        )

    sub768 = lax.broadcasted_iota(jnp.int32, (SLOTS, SITES, LANES), 1) + LANES * (
        lax.broadcasted_iota(jnp.int32, (SLOTS, SITES, LANES), 0)
    )
    sub768 = sub768.astype(F32).reshape(SLOTS * SITES, LANES)

    def scatter_hots(columns, which, col_hot):
        row = columns.T[which : which + 1, :]
        hot = jnp.where(
            sub768 == jnp.broadcast_to(row, (SLOTS * SITES, LANES)), 1.0, 0.0
        ).astype(BF16)
        return jnp.concatenate([hot, hot], axis=1), jnp.concatenate([col_hot, col_hot], axis=0)

    def scatter(row_hots, col_hots, row_data, col_re, col_im):
        high, low = split_pair(row_data)
        by_row = mxu(row_hots, jnp.concatenate([high, low], axis=0))
        turned = jnp.concatenate([col_re.T[:SITES], col_im.T[:SITES]], axis=0)
        high, low = split_pair(turned)
        by_col = mxu(jnp.concatenate([high, low], axis=1), col_hots)
        return by_row, by_col

    def block_of(parts, a):
        by_row, by_col = parts
        lanes = slice(a * LANES, (a + 1) * LANES)
        return by_row[a * SITES : (a + 1) * SITES] + jnp.concatenate(
            [by_col[:SITES, lanes], by_col[SITES:, lanes]], axis=1
        )

    asked_hots = scatter_hots(asked, 2, asked_col_hot)
    own_hots = scatter_hots(own, 0, own_col_hot)
    received(up_in_tiles, 8, 1, has_upper)
    row_re, row_im, col_re, col_im = get_tiles(up_in)
    parts = scatter(*asked_hots, jnp.concatenate([row_im, -row_re], axis=1), -col_im, col_re)
    for a in range(SLOTS):
        total[a * SITES : (a + 1) * SITES, :] += block_of(parts, a)

    received(reply_in_tiles, 8, 2, has_lower)
    row_re, row_im, col_re, col_im = get_tiles(reply_in)
    shared = jnp.broadcast_to(own[:, 4:5], (LANES, LANES))
    turn = jnp.broadcast_to(own[:, 5:6], (LANES, LANES))
    parts = scatter(
        *own_hots,
        jnp.concatenate([shared * row_re + turn * row_im, shared * row_im - turn * row_re], axis=1),
        shared * col_re - turn * col_im,
        shared * col_im + turn * col_re,
    )
    for a in range(SLOTS):
        value = total[a * SITES : (a + 1) * SITES, :] + block_of(parts, a)
        even_re, odd_re = value[:HALF, :LANES], value[HALF:, :LANES]
        even_im, odd_im = value[:HALF, LANES:], value[HALF:, LANES:]
        even_im = pltpu.roll(even_im, 96, 1)
        odd_re = pltpu.roll(odd_re, 64, 1)
        odd_im = pltpu.roll(odd_im, 32, 1)
        result[pl.ds(a, HALF, stride=24), :] = jnp.where(lane48 < SITES, even_re, even_im)
        result[pl.ds(8 + a, HALF, stride=24), :] = jnp.where(lane48 < 64, even_im, odd_re)
        result[pl.ds(16 + a, HALF, stride=24), :] = jnp.where(lane48 < 32, odd_re, odd_im)
    sent(tag_in_tiles, 2, 0, has_lower)
    sent(up_in_tiles, 8, 1, has_lower)
    sent(reply_in_tiles, 8, 2, has_upper)


def on_device(
    section_state,
    coupling,
    site_energy,
    bath_rate,
    bath_strength,
    bath_of_site,
    quanta,
    send_list,
    dest_slot,
):
    slots, width = section_state.shape
    chunks = width // LANES
    tiled = section_state.reshape(slots, chunks, LANES).transpose(1, 0, 2).reshape(-1, LANES)
    operands = (
        tiled,
        coupling,
        site_energy.reshape(1, SITES),
        bath_rate.reshape(1, SITES),
        bath_strength.reshape(1, SITES),
        bath_of_site.reshape(1, SITES),
        quanta.T,
        send_list,
        dest_slot,
    )
    tile_buffer = pltpu.VMEM((TILES * 8, LANES), F32)
    out = pl.pallas_call(
        kernel,
        out_shape=pltpu.VMEM(tiled.shape, F32),
        in_specs=[pl.BlockSpec(memory_space=pltpu.HBM)] * 9,
        out_specs=pl.BlockSpec(memory_space=pltpu.VMEM),
        scratch_shapes=[
            pltpu.VMEM(tiled.shape, F32),
            pltpu.VMEM((SITES, SITES), F32),
            pltpu.VMEM((3, 1, SITES), F32),
            pltpu.VMEM((1, SITES), jnp.int32),
            pltpu.VMEM((DEPTH, SLOTS), jnp.int32),
            pltpu.VMEM((1, LANES), jnp.int32),
            pltpu.VMEM((1, LANES), jnp.int32),
            tile_buffer,
            tile_buffer,
            tile_buffer,
            tile_buffer,
            tile_buffer,
            tile_buffer,
            pltpu.VMEM((LANES, LANES), F32),
            pltpu.VMEM((LANES, LANES), F32),
            pltpu.VMEM((SLOTS * LANES, 2 * LANES), BF16),
            pltpu.VMEM((SLOTS * LANES, 2 * LANES), BF16),
            pltpu.VMEM((SLOTS * LANES, 2 * LANES), BF16),
            pltpu.VMEM((SLOTS * LANES, 2 * LANES), BF16),
            pltpu.VMEM((SLOTS * SITES, 2 * LANES), F32),
            pltpu.SemaphoreType.DMA,
            pltpu.SemaphoreType.DMA((8,)),
            pltpu.SemaphoreType.DMA((3,)),
            pltpu.SemaphoreType.DMA((6,)),
        ],
        compiler_params=pltpu.CompilerParams(
            collective_id=0, has_side_effects=True, vmem_limit_bytes=32 * 1024 * 1024
        ),
    )(*[pltpu.with_memory_space_constraint(value, pltpu.HBM) for value in operands])
    return out.reshape(chunks, slots, LANES).transpose(1, 0, 2).reshape(slots, width)


def solution(mesh):
    return jax.shard_map(
        on_device,
        mesh=mesh,
        in_specs=(
            P(("tier", "aux"), None),
            P(),
            P(),
            P(),
            P(),
            P(),
            P(("tier", "aux"), None),
            P(("tier", "aux"), None),
            P(("tier", "aux"), None),
        ),
        out_specs=P(("tier", "aux"), None),
        check_vma=False,
    )
```

```python
import functools

import jax
import jax.numpy as jnp
from jax import lax
from jax.experimental import pallas as pl
from jax.experimental.pallas import tpu as pltpu
from jax.sharding import PartitionSpec as P

MESH = pl.DeviceIdType.MESH
F32 = jnp.float32
BF16 = jnp.bfloat16
SITES = 96
HALF = 48
SLOTS = 8
DEPTH = 4
PIECES = 3
PEERS = 32
TILES = 2 * PEERS
LANES = 128
TIERS = 8


def routes():
    found = [
        (across, dy, dx, dc)
        for across in range(2)
        for dy in range(4)
        for dx in range(4)
        for dc in range(2)
        if (across, dy, dx, dc) != (0, 0, 0, 0)
    ]
    return sorted(found, key=lambda s: (-(s[0] + min(s[1], 4 - s[1]) + min(s[2], 4 - s[2])), -s[3]))


ROUTES = routes()


def split_pair(value):
    high = value.astype(BF16)
    return high, (value - high.astype(F32)).astype(BF16)


def mxu(left, right):
    return jnp.dot(left, right, preferred_element_type=F32)


def kernel(
    state_hbm,
    coupling_hbm,
    energy_hbm,
    rate_hbm,
    strength_hbm,
    bath_hbm,
    quanta_hbm,
    send_hbm,
    dest_hbm,
    result,
    raw,
    coupling_v,
    table_v,
    bath_v,
    quanta_v,
    send_v,
    dest_v,
    tag_out,
    tag_in,
    up_out,
    up_in,
    reply_out,
    reply_in,
    tag_cols,
    own_cols,
    rows_hi,
    rows_lo,
    natural,
    table_hi,
    table_lo,
    total,
    load_sem,
    small_sem,
    send_sem,
    recv_sem,
):
    tier = lax.axis_index("tier")
    peer = lax.axis_index("aux")
    my_y = peer // 8
    my_x = lax.rem(peer, 8) // 2
    my_c = lax.rem(peer, 2)

    def partner(dy, dx, dc):
        return lax.rem(my_y + dy, 4) * 8 + lax.rem(my_x + dx, 4) * 2 + lax.rem(my_c + dc, 2)

    barrier = pltpu.get_barrier_semaphore()

    def greet(up, dy, dx, dc):
        pl.semaphore_signal(
            barrier,
            inc=1,
            device_id=(tier + up, partner(dy, dx, dc)),
            device_id_type=MESH,
        )

    def farthest_first(act, allowed):
        @pl.when(allowed)
        def _():
            for hop in ROUTES:
                act(*hop)

        @pl.when(jnp.logical_not(allowed))
        def _():
            for hop in ROUTES:
                if not hop[0]:
                    act(*hop)

    has_lower = tier > 0
    has_upper = tier < TIERS - 1
    farthest_first(greet, has_upper)

    small = [
        pltpu.make_async_copy(send_hbm, send_v, small_sem.at[0]),
        pltpu.make_async_copy(dest_hbm, dest_v, small_sem.at[1]),
        pltpu.make_async_copy(quanta_hbm, quanta_v, small_sem.at[2]),
        pltpu.make_async_copy(rate_hbm, table_v.at[0], small_sem.at[3]),
        pltpu.make_async_copy(strength_hbm, table_v.at[1], small_sem.at[4]),
        pltpu.make_async_copy(energy_hbm, table_v.at[2], small_sem.at[5]),
        pltpu.make_async_copy(bath_hbm, bath_v, small_sem.at[6]),
        pltpu.make_async_copy(coupling_hbm, coupling_v, small_sem.at[7]),
    ]
    for copy in small:
        copy.start()
    load = pltpu.make_async_copy(state_hbm, raw, load_sem)
    load.start()
    for copy in small:
        copy.wait()

    lane = lax.broadcasted_iota(jnp.int32, (1, LANES), 1)
    sub8 = lax.broadcasted_iota(jnp.int32, (SLOTS, LANES), 0)
    sub96 = lax.broadcasted_iota(jnp.int32, (SITES, LANES), 0)
    quanta = jnp.concatenate(
        [
            jnp.concatenate([quanta_v[...], jnp.zeros((DEPTH, LANES - SLOTS), jnp.int32)], axis=1),
            jnp.zeros((SLOTS - DEPTH, LANES), jnp.int32),
        ],
        axis=0,
    ).T[:SLOTS]

    def quanta_of(entry):
        slot = entry >> 2
        place = entry & 3
        hit = sub8 == jnp.broadcast_to(slot, (SLOTS, LANES))
        found = [
            jnp.sum(
                jnp.where(hit, jnp.broadcast_to(quanta[:, p : p + 1], (SLOTS, LANES)), 0),
                axis=0,
                keepdims=True,
            )
            for p in range(DEPTH)
        ]
        site = found[3]
        for p in range(DEPTH - 1):
            site = jnp.where(place == p, found[p], site)
        count = sum((found[p] == site).astype(F32) for p in range(DEPTH))
        return slot, site, count

    pad = jnp.zeros((1, LANES - SITES), F32)
    base = jnp.concatenate(
        [
            jnp.concatenate([bath_v[...].astype(F32), pad], axis=1),
            jnp.concatenate([table_v[0], pad], axis=1),
            jnp.concatenate([table_v[1], pad], axis=1),
            jnp.concatenate([table_v[2], pad], axis=1),
            jnp.zeros((LANES - 4, LANES), F32),
        ],
        axis=0,
    ).T
    bath_col = base[:SITES, 0:1]
    rate_col = base[:SITES, 1:2]
    strength_col = base[:SITES, 2:3]
    sub96f = sub96.astype(F32)

    def look_up(site, columns):
        hit = sub96 == jnp.broadcast_to(site, (SITES, LANES))
        bath = jnp.sum(
            jnp.where(hit, jnp.broadcast_to(bath_col, (SITES, LANES)), 0.0), axis=0, keepdims=True
        )
        hit = sub96f == jnp.broadcast_to(bath, (SITES, LANES))
        return [
            jnp.sum(
                jnp.where(hit, jnp.broadcast_to(column, (SITES, LANES)), 0.0), axis=0, keepdims=True
            )
            for column in columns
        ]

    entry = send_v[...]
    slot, site, weight = quanta_of(jnp.maximum(entry, 0))
    group = lane // (LANES // 2)
    usable = (entry >= 0) & (site >= 0) & (tier - group >= 0)
    strength_l, rate_l = look_up(site, [strength_col, rate_col])
    lower = dest_v[...]

    def marked(value):
        return jnp.where(usable, value, -1).astype(F32)

    tag_cols[...] = jnp.broadcast_to(marked(lower * SITES + site), (LANES, LANES)).T
    for c in range(2):
        tag_out[pl.ds(c, TILES, stride=8), :] = tag_cols[pl.ds(c, TILES, stride=2), :]
    tags = jnp.concatenate(
        [
            marked(slot * SITES + site),
            jnp.where(usable, -weight * (strength_l * rate_l), 0.0),
            jnp.where(usable, weight * strength_l, 0.0),
            jnp.zeros((LANES - 3, LANES), F32),
        ],
        axis=0,
    ).T
    own_cols[...] = tags
    own = jnp.concatenate([own_cols[pl.ds(c, TILES, stride=2), :] for c in range(2)], axis=0)
    tag_tiles = tag_out.reshape(TILES, 8, LANES)
    tag_in_tiles = tag_in.reshape(TILES, 8, LANES)
    up_tiles = up_out.reshape(TILES, 8, LANES)
    up_in_tiles = up_in.reshape(TILES, 8, LANES)
    reply_tiles = reply_out.reshape(TILES, 8, LANES)
    reply_in_tiles = reply_in.reshape(TILES, 8, LANES)

    def exchange(source, target, rows, which, step_tier, allowed):
        def send(across, dy, dx, dc):
            q = partner(dy, dx, dc)
            pltpu.make_async_remote_copy(
                source.at[PEERS * across + q, pl.ds(0, rows)],
                target.at[PEERS * across + peer, pl.ds(0, rows)],
                send_sem.at[which],
                recv_sem.at[2 * which + across],
                device_id=(tier + step_tier * across, q),
                device_id_type=MESH,
            ).start()

        farthest_first(send, allowed)

    def await_all(target, rows, which, near_sem, far_sem, far_allowed):
        block = target.at[pl.ds(0, PEERS - 1), pl.ds(0, rows)]
        pltpu.make_async_copy(block, block, near_sem).wait()

        @pl.when(far_allowed)
        def _():
            block = target.at[pl.ds(0, PEERS), pl.ds(0, rows)]
            pltpu.make_async_copy(block, block, far_sem).wait()

    def received(target, rows, which, far_allowed):
        await_all(target, rows, which, recv_sem.at[2 * which], recv_sem.at[2 * which + 1], far_allowed)

    def sent(target, rows, which, far_allowed):
        await_all(target, rows, which, send_sem.at[which], send_sem.at[which], far_allowed)

    self_row = pl.multiple_of(peer * 8, 8)
    tag_in[pl.ds(self_row, 8), :] = tag_out[pl.ds(self_row, 8), :]

    @pl.when(tier == TIERS - 1)
    def _():
        tag_in[PEERS * 8 :, :] = jnp.full((PEERS * 8, LANES), -1.0, F32)
        up_in[PEERS * 8 :, :] = jnp.zeros((PEERS * 8, LANES), F32)

    @pl.when(tier == 0)
    def _():
        reply_in[PEERS * 8 :, :] = jnp.zeros((PEERS * 8, LANES), F32)

    pl.semaphore_wait(barrier, jnp.where(has_lower, 2 * PEERS - 1, PEERS - 1))

    exchange(tag_tiles, tag_in_tiles, 2, 0, -1, has_lower)

    load.wait()
    lane48 = lax.broadcasted_iota(jnp.int32, (HALF, LANES), 1)
    lane96 = lax.broadcasted_iota(jnp.int32, (SITES, LANES), 1)
    zero48 = jnp.zeros((HALF, LANES), F32)
    gap = jnp.zeros((LANES - SITES, LANES), F32)
    ok = lane48 < SITES
    for a in range(SLOTS):
        t0 = raw[pl.ds(a, HALF, stride=24), :]
        t1 = raw[pl.ds(8 + a, HALF, stride=24), :]
        t2 = raw[pl.ds(16 + a, HALF, stride=24), :]
        odd0 = jnp.where(lane48 < 64, pltpu.roll(t1, 64, 1), pltpu.roll(t2, 64, 1))
        odd1 = pltpu.roll(t2, 64, 1)
        left_at, right_at = a * SITES, (SLOTS + a) * SITES
        natural[pl.ds(left_at, HALF, stride=2), :] = t0
        natural[pl.ds(right_at, HALF, stride=2), :] = t1
        natural[pl.ds(left_at + 1, HALF, stride=2), :] = odd0
        natural[pl.ds(right_at + 1, HALF, stride=2), :] = odd1
        even_im = jnp.where(
            lane48 < 32, pltpu.roll(t0, 32, 1), jnp.where(ok, pltpu.roll(t1, 32, 1), zero48)
        )
        odd_im = jnp.where(ok, pltpu.roll(t2, 96, 1), zero48)
        real = jnp.concatenate(
            [jnp.where(ok, t0, zero48), jnp.where(ok, odd0, zero48), gap], axis=0
        )
        imag = jnp.concatenate([even_im, odd_im, gap], axis=0)
        high, low = split_pair(jnp.concatenate([real, imag], axis=1))
        block = slice(a * LANES, (a + 1) * LANES)
        rows_hi[block, :] = high
        rows_lo[block, :] = low
        turned_re = pltpu.roll(real.T[:SITES], 64, 1)
        turned_im = pltpu.roll(imag.T[:SITES], 32, 1)
        block = slice(a * SITES, (a + 1) * SITES)
        high, low = split_pair(
            jnp.concatenate(
                [
                    natural[left_at : left_at + SITES, :],
                    jnp.where(
                        lane96 < 64, natural[right_at : right_at + SITES, :], turned_re
                    ),
                    jnp.where(lane96 < 32, turned_re, turned_im),
                ],
                axis=1,
            )
        )
        table_hi[block, :] = high
        table_lo[block, :] = low

    lane_f = lax.broadcasted_iota(jnp.int32, (LANES, LANES), 1).astype(F32)

    def one_hot(index, chunks):
        return jnp.concatenate(
            [
                jnp.where(lane_f == index - float(LANES * k), 1.0, 0.0).astype(BF16)
                for k in range(chunks)
            ],
            axis=1,
        )

    def gather(index):
        hot = one_hot(index, SLOTS * SITES // LANES)
        return mxu(hot, table_hi[...]) + mxu(hot, table_lo[...])

    def put_tiles(target, packed):
        for c in range(2):
            for k in range(PIECES):
                target[pl.ds(PIECES * c + k, TILES, stride=8), :] = packed[
                    c * TILES : (c + 1) * TILES, k * LANES : (k + 1) * LANES
                ]

    def get_tiles(source):
        def piece(k):
            return jnp.concatenate(
                [source[pl.ds(PIECES * c + k, TILES, stride=8), :] for c in range(2)], axis=0
            )

        first, middle, last = piece(0), piece(1), piece(2)
        row_im = jnp.where(lane_f < 32.0, pltpu.roll(first, 32, 1), pltpu.roll(middle, 32, 1))
        col_re = jnp.where(lane_f < 64.0, pltpu.roll(middle, 64, 1), pltpu.roll(last, 64, 1))
        return first, row_im, col_re, pltpu.roll(last, 96, 1)

    own_index = jnp.broadcast_to(own[:, 0:1], (LANES, LANES))
    put_tiles(up_out, gather(own_index))
    up_in[pl.ds(self_row, 8), :] = up_out[pl.ds(self_row, 8), :]
    exchange(up_tiles, up_in_tiles, 2 * PIECES, 1, -1, has_lower)

    received(tag_in_tiles, 2, 0, has_upper)
    asked = jnp.concatenate([tag_in[pl.ds(c, TILES, stride=8), :] for c in range(2)], axis=0)
    put_tiles(reply_out, gather(asked))
    exchange(reply_tiles, reply_in_tiles, 2 * PIECES, 2, 1, has_upper)
    reply_in[pl.ds(self_row, 8), :] = reply_out[pl.ds(self_row, 8), :]

    diagonal = lax.broadcasted_iota(jnp.int32, (SITES, SITES), 0) == lax.broadcasted_iota(
        jnp.int32, (SITES, SITES), 1
    )
    coupling = coupling_v[...]
    hamilton = (coupling + coupling.T) * 0.5 + jnp.where(
        diagonal, jnp.broadcast_to(base[:SITES, 3:4], (SITES, SITES)), 0.0
    )
    row_id = lax.broadcasted_iota(jnp.int32, (SITES, SITES), 0)
    site_of_row = jnp.where(row_id < HALF, 2 * row_id, 2 * (row_id - HALF) + 1)
    chooser = jnp.where(
        site_of_row == lax.broadcasted_iota(jnp.int32, (SITES, SITES), 1), 1.0, 0.0
    ).astype(BF16)
    h_hi, h_lo = split_pair(hamilton)
    p_hi = mxu(chooser, h_hi).astype(BF16)
    p_lo = mxu(chooser, h_lo).astype(BF16)
    p_hi = mxu(p_hi, chooser.T).astype(BF16)
    p_lo = mxu(p_lo, chooser.T).astype(BF16)
    gap_r = jnp.zeros((SITES, LANES - SITES), BF16)
    left_hi = jnp.concatenate([p_hi, gap_r], axis=1)
    left_lo = jnp.concatenate([p_lo, gap_r], axis=1)
    gap_b = jnp.zeros((LANES - SITES, LANES), BF16)

    def turned_pair(h):
        square = jnp.concatenate([jnp.concatenate([h, gap_r], axis=1), gap_b], axis=0)
        empty = jnp.zeros((LANES, LANES), BF16)
        return jnp.concatenate(
            [
                jnp.concatenate([empty, square], axis=1),
                jnp.concatenate([-square, empty], axis=1),
            ],
            axis=0,
        )

    right_hi = turned_pair(h_hi)
    right_lo = turned_pair(h_lo)

    edge_slot, edge_site, _ = quanta_of(jnp.minimum(lane, SLOTS * DEPTH - 1))
    (edge_rate,) = look_up(edge_site, [rate_col])
    edge_rate = jnp.where((lane < SLOTS * DEPTH) & (edge_site >= 0), edge_rate, 0.0)
    damping = jnp.sum(
        jnp.where(
            sub8 == jnp.broadcast_to(edge_slot, (SLOTS, LANES)),
            jnp.broadcast_to(edge_rate, (SLOTS, LANES)),
            0.0,
        ),
        axis=1,
        keepdims=True,
    )

    for a in range(SLOTS):
        z_hi = rows_hi[a * LANES : (a + 1) * LANES, :]
        z_lo = rows_lo[a * LANES : (a + 1) * LANES, :]
        left = mxu(left_hi, z_hi) + mxu(left_hi, z_lo) + mxu(left_lo, z_hi)
        z_hi = z_hi[:SITES]
        z_lo = z_lo[:SITES]
        right = mxu(z_hi, right_hi) + mxu(z_lo, right_hi) + mxu(z_hi, right_lo)
        z = z_hi.astype(F32) + z_lo.astype(F32)
        total[a * SITES : (a + 1) * SITES, :] = (
            jnp.concatenate([left[:, LANES:], -left[:, :LANES]], axis=1)
            + right
            - damping[a : a + 1, 0:1] * z
        )

    sub768 = lax.broadcasted_iota(jnp.int32, (SLOTS * SITES, LANES), 0).astype(F32)

    def scatter_hots(index):
        slot_f = jnp.floor((index + 0.5) * (1.0 / SITES))
        site_f = index - float(SITES) * slot_f
        half = jnp.floor(site_f * 0.5)
        in_order = float(SITES) * slot_f + half + float(HALF) * (site_f - 2.0 * half)
        row_hot = jnp.where(
            sub768 == jnp.broadcast_to(in_order.T[0:1], (SLOTS * SITES, LANES)), 1.0, 0.0
        ).astype(BF16)
        col_hot = one_hot(float(LANES) * slot_f + site_f, SLOTS)
        return jnp.concatenate([row_hot, row_hot], axis=1), jnp.concatenate([col_hot, col_hot], axis=0)

    def scatter(row_hots, col_hots, row_data, col_re, col_im):
        high, low = split_pair(row_data)
        by_row = mxu(row_hots, jnp.concatenate([high, low], axis=0))
        turned = jnp.concatenate([col_re.T[:SITES], col_im.T[:SITES]], axis=0)
        high, low = split_pair(turned)
        by_col = mxu(jnp.concatenate([high, low], axis=1), col_hots)
        return by_row, by_col

    def block_of(parts, a):
        by_row, by_col = parts
        lanes = slice(a * LANES, (a + 1) * LANES)
        return by_row[a * SITES : (a + 1) * SITES] + jnp.concatenate(
            [by_col[:SITES, lanes], by_col[SITES:, lanes]], axis=1
        )

    asked_hots = scatter_hots(asked)
    own_hots = scatter_hots(own_index)
    received(up_in_tiles, 2 * PIECES, 1, has_upper)
    row_re, row_im, col_re, col_im = get_tiles(up_in)
    parts = scatter(*asked_hots, jnp.concatenate([row_im, -row_re], axis=1), -col_im, col_re)
    for a in range(SLOTS):
        total[a * SITES : (a + 1) * SITES, :] += block_of(parts, a)

    received(reply_in_tiles, 2 * PIECES, 2, has_lower)
    row_re, row_im, col_re, col_im = get_tiles(reply_in)
    shared = jnp.broadcast_to(own[:, 1:2], (LANES, LANES))
    turn = jnp.broadcast_to(own[:, 2:3], (LANES, LANES))
    parts = scatter(
        *own_hots,
        jnp.concatenate([shared * row_re + turn * row_im, shared * row_im - turn * row_re], axis=1),
        shared * col_re - turn * col_im,
        shared * col_im + turn * col_re,
    )
    for a in range(SLOTS):
        value = total[a * SITES : (a + 1) * SITES, :] + block_of(parts, a)
        even_re, odd_re = value[:HALF, :LANES], value[HALF:, :LANES]
        even_im, odd_im = value[:HALF, LANES:], value[HALF:, LANES:]
        even_im = pltpu.roll(even_im, 96, 1)
        odd_re = pltpu.roll(odd_re, 64, 1)
        odd_im = pltpu.roll(odd_im, 32, 1)
        result[pl.ds(a, HALF, stride=24), :] = jnp.where(lane48 < SITES, even_re, even_im)
        result[pl.ds(8 + a, HALF, stride=24), :] = jnp.where(lane48 < 64, even_im, odd_re)
        result[pl.ds(16 + a, HALF, stride=24), :] = jnp.where(lane48 < 32, odd_re, odd_im)
    sent(tag_in_tiles, 2, 0, has_lower)
    sent(up_in_tiles, 2 * PIECES, 1, has_lower)
    sent(reply_in_tiles, 2 * PIECES, 2, has_upper)


def on_device(
    section_state,
    coupling,
    site_energy,
    bath_rate,
    bath_strength,
    bath_of_site,
    quanta,
    send_list,
    dest_slot,
):
    slots, width = section_state.shape
    chunks = width // LANES
    tiled = section_state.reshape(slots, chunks, LANES).transpose(1, 0, 2).reshape(-1, LANES)
    operands = (
        tiled,
        coupling,
        site_energy.reshape(1, SITES),
        bath_rate.reshape(1, SITES),
        bath_strength.reshape(1, SITES),
        bath_of_site.reshape(1, SITES),
        quanta.T,
        send_list,
        dest_slot,
    )
    tile_buffer = pltpu.VMEM((TILES * 8, LANES), F32)
    out = pl.pallas_call(
        kernel,
        out_shape=pltpu.VMEM(tiled.shape, F32),
        in_specs=[pl.BlockSpec(memory_space=pltpu.HBM)] * 9,
        out_specs=pl.BlockSpec(memory_space=pltpu.VMEM),
        scratch_shapes=[
            pltpu.VMEM(tiled.shape, F32),
            pltpu.VMEM((SITES, SITES), F32),
            pltpu.VMEM((3, 1, SITES), F32),
            pltpu.VMEM((1, SITES), jnp.int32),
            pltpu.VMEM((DEPTH, SLOTS), jnp.int32),
            pltpu.VMEM((1, LANES), jnp.int32),
            pltpu.VMEM((1, LANES), jnp.int32),
            tile_buffer,
            tile_buffer,
            tile_buffer,
            tile_buffer,
            tile_buffer,
            tile_buffer,
            pltpu.VMEM((LANES, LANES), F32),
            pltpu.VMEM((LANES, LANES), F32),
            pltpu.VMEM((SLOTS * LANES, 2 * LANES), BF16),
            pltpu.VMEM((SLOTS * LANES, 2 * LANES), BF16),
            pltpu.VMEM((2 * SLOTS * SITES, LANES), F32),
            pltpu.VMEM((SLOTS * SITES, PIECES * LANES), BF16),
            pltpu.VMEM((SLOTS * SITES, PIECES * LANES), BF16),
            pltpu.VMEM((SLOTS * SITES, 2 * LANES), F32),
            pltpu.SemaphoreType.DMA,
            pltpu.SemaphoreType.DMA((8,)),
            pltpu.SemaphoreType.DMA((3,)),
            pltpu.SemaphoreType.DMA((6,)),
        ],
        compiler_params=pltpu.CompilerParams(
            collective_id=0, has_side_effects=True, vmem_limit_bytes=32 * 1024 * 1024
        ),
    )(*[pltpu.with_memory_space_constraint(value, pltpu.HBM) for value in operands])
    return out.reshape(chunks, slots, LANES).transpose(1, 0, 2).reshape(slots, width)


def solution(mesh):
    return jax.shard_map(
        on_device,
        mesh=mesh,
        in_specs=(
            P(("tier", "aux"), None),
            P(),
            P(),
            P(),
            P(),
            P(),
            P(("tier", "aux"), None),
            P(("tier", "aux"), None),
            P(("tier", "aux"), None),
        ),
        out_specs=P(("tier", "aux"), None),
        check_vma=False,
    )
```

```python
import functools

import jax
import jax.numpy as jnp
from jax import lax
from jax.experimental import pallas as pl
from jax.experimental.pallas import tpu as pltpu
from jax.sharding import PartitionSpec as P

MESH = pl.DeviceIdType.MESH
F32 = jnp.float32
BF16 = jnp.bfloat16
SITES = 96
HALF = 48
SLOTS = 8
DEPTH = 4
PIECES = 3
PEERS = 32
TILES = 2 * PEERS
LANES = 128
TIERS = 8


def routes():
    found = [
        (across, dy, dx, dc)
        for across in range(2)
        for dy in range(4)
        for dx in range(4)
        for dc in range(2)
        if (across, dy, dx, dc) != (0, 0, 0, 0)
    ]
    return sorted(found, key=lambda s: (-(s[0] + min(s[1], 4 - s[1]) + min(s[2], 4 - s[2])), -s[3]))


ROUTES = routes()


def split_pair(value):
    high = value.astype(BF16)
    return high, (value - high.astype(F32)).astype(BF16)


def mxu(left, right):
    return jnp.dot(left, right, preferred_element_type=F32)


def kernel(
    state_hbm,
    coupling_hbm,
    energy_hbm,
    rate_hbm,
    strength_hbm,
    bath_hbm,
    quanta_hbm,
    send_hbm,
    dest_hbm,
    result,
    raw,
    coupling_v,
    table_v,
    bath_v,
    quanta_v,
    send_v,
    dest_v,
    tag_out,
    tag_in,
    up_out,
    up_in,
    reply_out,
    reply_in,
    tag_cols,
    own_cols,
    rows_hi,
    rows_lo,
    natural,
    table_hi,
    table_lo,
    total,
    load_sem,
    small_sem,
    send_sem,
    recv_sem,
):
    tier = lax.axis_index("tier")
    peer = lax.axis_index("aux")
    my_y = peer // 8
    my_x = lax.rem(peer, 8) // 2
    my_c = lax.rem(peer, 2)

    at_y = [lax.rem(my_y + d, 4) * 8 for d in range(4)]
    at_x = [lax.rem(my_x + d, 4) * 2 for d in range(4)]
    at_c = [my_c, 1 - my_c]

    def partner(dy, dx, dc):
        return at_y[dy % 4] + at_x[dx % 4] + at_c[dc]

    barrier = pltpu.get_barrier_semaphore()

    def greet(up, dy, dx, dc):
        pl.semaphore_signal(
            barrier,
            inc=1,
            device_id=(tier + up, partner(dy, dx, dc)),
            device_id_type=MESH,
        )

    def farthest_first(act, allowed, chosen=(0, 1)):
        if chosen == (0,):
            for hop in ROUTES:
                if not hop[0]:
                    act(*hop)
            return

        @pl.when(allowed)
        def _():
            for hop in ROUTES:
                if hop[0] in chosen:
                    act(*hop)

        if 0 not in chosen:
            return

        @pl.when(jnp.logical_not(allowed))
        def _():
            for hop in ROUTES:
                if not hop[0]:
                    act(*hop)

    has_lower = tier > 0
    has_upper = tier < TIERS - 1
    farthest_first(greet, has_upper)

    small = [
        pltpu.make_async_copy(send_hbm, send_v, small_sem.at[0]),
        pltpu.make_async_copy(dest_hbm, dest_v, small_sem.at[1]),
        pltpu.make_async_copy(quanta_hbm, quanta_v, small_sem.at[2]),
        pltpu.make_async_copy(rate_hbm, table_v.at[0], small_sem.at[3]),
        pltpu.make_async_copy(strength_hbm, table_v.at[1], small_sem.at[4]),
        pltpu.make_async_copy(energy_hbm, table_v.at[2], small_sem.at[5]),
        pltpu.make_async_copy(bath_hbm, bath_v, small_sem.at[6]),
        pltpu.make_async_copy(coupling_hbm, coupling_v, small_sem.at[7]),
    ]
    for copy in small:
        copy.start()
    load = pltpu.make_async_copy(state_hbm, raw, load_sem)
    load.start()
    for copy in small:
        copy.wait()

    lane = lax.broadcasted_iota(jnp.int32, (1, LANES), 1)
    sub8 = lax.broadcasted_iota(jnp.int32, (SLOTS, LANES), 0)
    sub96 = lax.broadcasted_iota(jnp.int32, (SITES, LANES), 0)
    quanta = jnp.concatenate(
        [
            jnp.concatenate([quanta_v[...], jnp.zeros((DEPTH, LANES - SLOTS), jnp.int32)], axis=1),
            jnp.zeros((SLOTS - DEPTH, LANES), jnp.int32),
        ],
        axis=0,
    ).T[:SLOTS]

    def quanta_of(entry):
        slot = entry >> 2
        place = entry & 3
        hit = sub8 == jnp.broadcast_to(slot, (SLOTS, LANES))
        found = [
            jnp.sum(
                jnp.where(hit, jnp.broadcast_to(quanta[:, p : p + 1], (SLOTS, LANES)), 0),
                axis=0,
                keepdims=True,
            )
            for p in range(DEPTH)
        ]
        site = found[3]
        for p in range(DEPTH - 1):
            site = jnp.where(place == p, found[p], site)
        count = sum((found[p] == site).astype(F32) for p in range(DEPTH))
        return slot, site, count

    pad = jnp.zeros((1, LANES - SITES), F32)
    base = jnp.concatenate(
        [
            jnp.concatenate([bath_v[...].astype(F32), pad], axis=1),
            jnp.concatenate([table_v[0], pad], axis=1),
            jnp.concatenate([table_v[1], pad], axis=1),
            jnp.concatenate([table_v[2], pad], axis=1),
            jnp.zeros((LANES - 4, LANES), F32),
        ],
        axis=0,
    ).T
    bath_col = base[:SITES, 0:1]
    rate_col = base[:SITES, 1:2]
    strength_col = base[:SITES, 2:3]
    sub96f = sub96.astype(F32)

    def look_up(site, columns):
        hit = sub96 == jnp.broadcast_to(site, (SITES, LANES))
        bath = jnp.sum(
            jnp.where(hit, jnp.broadcast_to(bath_col, (SITES, LANES)), 0.0), axis=0, keepdims=True
        )
        hit = sub96f == jnp.broadcast_to(bath, (SITES, LANES))
        return [
            jnp.sum(
                jnp.where(hit, jnp.broadcast_to(column, (SITES, LANES)), 0.0), axis=0, keepdims=True
            )
            for column in columns
        ]

    entry = send_v[...]
    slot, site, weight = quanta_of(jnp.maximum(entry, 0))
    group = lane // (LANES // 2)
    usable = (entry >= 0) & (site >= 0) & (tier - group >= 0)
    strength_l, rate_l = look_up(site, [strength_col, rate_col])
    lower = dest_v[...]

    def marked(value):
        return jnp.where(usable, value, -1).astype(F32)

    tag_cols[...] = jnp.broadcast_to(marked(lower * SITES + site), (LANES, LANES)).T
    left_half = lax.broadcasted_iota(jnp.int32, (TILES, LANES), 1) < TILES
    tag_out[pl.ds(0, TILES, stride=8), :] = jnp.where(
        left_half, tag_cols[pl.ds(0, TILES, stride=2), :], tag_cols[pl.ds(1, TILES, stride=2), :]
    )
    tags = jnp.concatenate(
        [
            marked(slot * SITES + site),
            jnp.where(usable, -weight * (strength_l * rate_l), 0.0),
            jnp.where(usable, weight * strength_l, 0.0),
            jnp.zeros((LANES - 3, LANES), F32),
        ],
        axis=0,
    ).T
    own_cols[...] = tags
    own = [
        jnp.concatenate(
            [own_cols[pl.ds(TILES * g + c, PEERS, stride=2), :] for c in range(2)], axis=0
        )
        for g in range(2)
    ]
    tag_tiles = tag_out.reshape(TILES, 8, LANES)
    tag_in_tiles = tag_in.reshape(TILES, 8, LANES)
    up_tiles = up_out.reshape(TILES, 8, LANES)
    up_in_tiles = up_in.reshape(TILES, 8, LANES)
    reply_tiles = reply_out.reshape(TILES, 8, LANES)
    reply_in_tiles = reply_in.reshape(TILES, 8, LANES)

    def exchange(source, target, rows, which, step_tier, allowed, chosen=(0, 1)):
        def send(across, dy, dx, dc):
            q = partner(dy, dx, dc)
            pltpu.make_async_remote_copy(
                source.at[PEERS * across + q, pl.ds(0, rows)],
                target.at[PEERS * across + peer, pl.ds(0, rows)],
                send_sem.at[which],
                recv_sem.at[2 * which + across],
                device_id=(tier + step_tier * across, q),
                device_id_type=MESH,
            ).start()

        farthest_first(send, allowed, chosen)

    def await_near(target, rows, semaphore):
        block = target.at[pl.ds(0, PEERS - 1), pl.ds(0, rows)]
        pltpu.make_async_copy(block, block, semaphore).wait()

    def await_far(target, rows, semaphore, allowed):
        @pl.when(allowed)
        def _():
            block = target.at[pl.ds(0, PEERS), pl.ds(0, rows)]
            pltpu.make_async_copy(block, block, semaphore).wait()

    def received_near(target, rows, which):
        await_near(target, rows, recv_sem.at[2 * which])

    def received_far(target, rows, which, allowed):
        await_far(target, rows, recv_sem.at[2 * which + 1], allowed)

    def sent(target, rows, which, allowed):
        await_near(target, rows, send_sem.at[which])
        await_far(target, rows, send_sem.at[which], allowed)

    self_row = pl.multiple_of(peer * 8, 8)
    tag_in[pl.ds(self_row, 8), :] = tag_out[pl.ds(self_row, 8), :]

    @pl.when(tier == TIERS - 1)
    def _():
        tag_in[PEERS * 8 :, :] = jnp.full((PEERS * 8, LANES), -1.0, F32)
        up_in[PEERS * 8 :, :] = jnp.zeros((PEERS * 8, LANES), F32)

    @pl.when(tier == 0)
    def _():
        reply_in[PEERS * 8 :, :] = jnp.zeros((PEERS * 8, LANES), F32)

    pl.semaphore_wait(barrier, jnp.where(has_lower, 2 * PEERS - 1, PEERS - 1))

    exchange(tag_tiles, tag_in_tiles, 1, 0, -1, has_lower)

    load.wait()
    lane48 = lax.broadcasted_iota(jnp.int32, (HALF, LANES), 1)
    lane96 = lax.broadcasted_iota(jnp.int32, (SITES, LANES), 1)
    zero48 = jnp.zeros((HALF, LANES), F32)
    gap = jnp.zeros((LANES - SITES, LANES), F32)
    ok = lane48 < SITES
    for a in range(SLOTS):
        t0 = raw[pl.ds(a, HALF, stride=24), :]
        t1 = raw[pl.ds(8 + a, HALF, stride=24), :]
        t2 = raw[pl.ds(16 + a, HALF, stride=24), :]
        odd0 = jnp.where(lane48 < 64, pltpu.roll(t1, 64, 1), pltpu.roll(t2, 64, 1))
        odd1 = pltpu.roll(t2, 64, 1)
        left_at, right_at = a * SITES, (SLOTS + a) * SITES
        natural[pl.ds(left_at, HALF, stride=2), :] = t0
        natural[pl.ds(right_at, HALF, stride=2), :] = t1
        natural[pl.ds(left_at + 1, HALF, stride=2), :] = odd0
        natural[pl.ds(right_at + 1, HALF, stride=2), :] = odd1
        even_im = jnp.where(
            lane48 < 32, pltpu.roll(t0, 32, 1), jnp.where(ok, pltpu.roll(t1, 32, 1), zero48)
        )
        odd_im = jnp.where(ok, pltpu.roll(t2, 96, 1), zero48)
        real = jnp.concatenate(
            [jnp.where(ok, t0, zero48), jnp.where(ok, odd0, zero48), gap], axis=0
        )
        imag = jnp.concatenate([even_im, odd_im, gap], axis=0)
        high, low = split_pair(jnp.concatenate([real, imag], axis=1))
        block = slice(a * LANES, (a + 1) * LANES)
        rows_hi[block, :] = high
        rows_lo[block, :] = low
        turned_re = pltpu.roll(real.T[:SITES], 64, 1)
        turned_im = pltpu.roll(imag.T[:SITES], 32, 1)
        block = slice(a * SITES, (a + 1) * SITES)
        high, low = split_pair(
            jnp.concatenate(
                [
                    natural[left_at : left_at + SITES, :],
                    jnp.where(
                        lane96 < 64, natural[right_at : right_at + SITES, :], turned_re
                    ),
                    jnp.where(lane96 < 32, turned_re, turned_im),
                ],
                axis=1,
            )
        )
        table_hi[block, :] = high
        table_lo[block, :] = low

    lane_f = lax.broadcasted_iota(jnp.int32, (LANES, LANES), 1).astype(F32)

    def one_hot(index, chunks):
        return jnp.concatenate(
            [
                jnp.where(lane_f[: index.shape[0]] == index - float(LANES * k), 1.0, 0.0).astype(BF16)
                for k in range(chunks)
            ],
            axis=1,
        )

    def gather(index):
        hot = one_hot(index, SLOTS * SITES // LANES)
        return mxu(hot, table_hi[...]) + mxu(hot, table_lo[...])

    def put_tiles(target, g, packed):
        for c in range(2):
            for k in range(PIECES):
                target[pl.ds(PEERS * 8 * g + PIECES * c + k, PEERS, stride=8), :] = packed[
                    c * PEERS : (c + 1) * PEERS, k * LANES : (k + 1) * LANES
                ]

    lane_h = lane_f[: 2 * PEERS]

    def get_tiles(source, g):
        def piece(k):
            return jnp.concatenate(
                [
                    source[pl.ds(PEERS * 8 * g + PIECES * c + k, PEERS, stride=8), :]
                    for c in range(2)
                ],
                axis=0,
            )

        first, middle, last = piece(0), piece(1), piece(2)
        row_im = jnp.where(lane_h < 32.0, pltpu.roll(first, 32, 1), pltpu.roll(middle, 32, 1))
        col_re = jnp.where(lane_h < 64.0, pltpu.roll(middle, 64, 1), pltpu.roll(last, 64, 1))
        return first, row_im, col_re, pltpu.roll(last, 96, 1)

    own_index = [jnp.broadcast_to(own[g][:, 0:1], (TILES, LANES)) for g in range(2)]
    packed = gather(jnp.concatenate(own_index, axis=0))
    for g in range(2):
        put_tiles(up_out, g, packed[g * TILES : (g + 1) * TILES])
    up_in[pl.ds(self_row, 8), :] = up_out[pl.ds(self_row, 8), :]
    exchange(up_tiles, up_in_tiles, 2 * PIECES, 1, -1, has_lower)

    asked = []
    for g in range(2):
        if g == 0:
            received_near(tag_in_tiles, 1, 0)
        else:
            received_far(tag_in_tiles, 1, 0, has_upper)
        both = tag_in[pl.ds(PEERS * 8 * g, PEERS, stride=8), :]
        swapped = pltpu.roll(both, TILES, 1)
        index = jnp.concatenate(
            [
                jnp.where(left_half[:PEERS], both, swapped),
                jnp.where(left_half[:PEERS], swapped, both),
            ],
            axis=0,
        )
        asked.append(index)
        put_tiles(reply_out, g, gather(index))
        exchange(reply_tiles, reply_in_tiles, 2 * PIECES, 2, 1, has_upper if g else True, (g,))
    reply_in[pl.ds(self_row, 8), :] = reply_out[pl.ds(self_row, 8), :]

    diagonal = lax.broadcasted_iota(jnp.int32, (SITES, SITES), 0) == lax.broadcasted_iota(
        jnp.int32, (SITES, SITES), 1
    )
    coupling = coupling_v[...]
    hamilton = (coupling + coupling.T) * 0.5 + jnp.where(
        diagonal, jnp.broadcast_to(base[:SITES, 3:4], (SITES, SITES)), 0.0
    )
    row_id = lax.broadcasted_iota(jnp.int32, (SITES, SITES), 0)
    site_of_row = jnp.where(row_id < HALF, 2 * row_id, 2 * (row_id - HALF) + 1)
    chooser = jnp.where(
        site_of_row == lax.broadcasted_iota(jnp.int32, (SITES, SITES), 1), 1.0, 0.0
    ).astype(BF16)
    h_hi, h_lo = split_pair(hamilton)
    p_hi = mxu(chooser, h_hi).astype(BF16)
    p_lo = mxu(chooser, h_lo).astype(BF16)
    p_hi = mxu(p_hi, chooser.T).astype(BF16)
    p_lo = mxu(p_lo, chooser.T).astype(BF16)
    gap_r = jnp.zeros((SITES, LANES - SITES), BF16)
    left_hi = jnp.concatenate([p_hi, gap_r], axis=1)
    left_lo = jnp.concatenate([p_lo, gap_r], axis=1)
    gap_b = jnp.zeros((LANES - SITES, LANES), BF16)

    def turned_pair(h):
        square = jnp.concatenate([jnp.concatenate([h, gap_r], axis=1), gap_b], axis=0)
        empty = jnp.zeros((LANES, LANES), BF16)
        return jnp.concatenate(
            [
                jnp.concatenate([empty, square], axis=1),
                jnp.concatenate([-square, empty], axis=1),
            ],
            axis=0,
        )

    right_hi = turned_pair(h_hi)
    right_lo = turned_pair(h_lo)

    edge_slot, edge_site, _ = quanta_of(jnp.minimum(lane, SLOTS * DEPTH - 1))
    (edge_rate,) = look_up(edge_site, [rate_col])
    edge_rate = jnp.where((lane < SLOTS * DEPTH) & (edge_site >= 0), edge_rate, 0.0)
    damping = jnp.sum(
        jnp.where(
            sub8 == jnp.broadcast_to(edge_slot, (SLOTS, LANES)),
            jnp.broadcast_to(edge_rate, (SLOTS, LANES)),
            0.0,
        ),
        axis=1,
        keepdims=True,
    )

    for a in range(SLOTS):
        z_hi = rows_hi[a * LANES : (a + 1) * LANES, :]
        z_lo = rows_lo[a * LANES : (a + 1) * LANES, :]
        left = mxu(left_hi, z_hi) + mxu(left_hi, z_lo) + mxu(left_lo, z_hi)
        z_hi = z_hi[:SITES]
        z_lo = z_lo[:SITES]
        right = mxu(z_hi, right_hi) + mxu(z_lo, right_hi) + mxu(z_hi, right_lo)
        z = z_hi.astype(F32) + z_lo.astype(F32)
        total[a * SITES : (a + 1) * SITES, :] = (
            jnp.concatenate([left[:, LANES:], -left[:, :LANES]], axis=1)
            + right
            - damping[a : a + 1, 0:1] * z
        )

    sub768 = lax.broadcasted_iota(jnp.int32, (SLOTS * SITES, LANES), 0).astype(F32)

    def scatter_hots(index):
        slot_f = jnp.floor((index + 0.5) * (1.0 / SITES))
        site_f = index - float(SITES) * slot_f
        half = jnp.floor(site_f * 0.5)
        in_order = float(SITES) * slot_f + half + float(HALF) * (site_f - 2.0 * half)
        row_hot = jnp.where(
            sub768 == jnp.broadcast_to(in_order.T[0:1], (SLOTS * SITES, LANES)), 1.0, 0.0
        ).astype(BF16)
        col_hot = one_hot(float(LANES) * slot_f + site_f, SLOTS)
        return row_hot, col_hot

    def scatter(row_hots, col_hots, row_data, col_re, col_im):
        high, low = split_pair(row_data)
        by_row = mxu(row_hots, jnp.concatenate([high, low], axis=0))
        turned = []
        for column in (col_re, col_im):
            high, low = split_pair(column)
            stacked = jnp.concatenate([high.astype(F32), low.astype(F32)], axis=0)
            turned.append(stacked.T[:SITES].astype(BF16))
        by_col = mxu(jnp.concatenate(turned, axis=0), col_hots)
        return by_row, by_col

    def block_of(parts, a):
        by_row, by_col = parts
        lanes = slice(a * LANES, (a + 1) * LANES)
        return by_row[a * SITES : (a + 1) * SITES] + jnp.concatenate(
            [by_col[:SITES, lanes], by_col[SITES:, lanes]], axis=1
        )

    def twice(index):
        return jnp.concatenate([index, index], axis=0)

    for g in range(2):
        hots = scatter_hots(twice(asked[g]))
        if g == 0:
            received_near(up_in_tiles, 2 * PIECES, 1)
        else:
            received_far(up_in_tiles, 2 * PIECES, 1, has_upper)
        row_re, row_im, col_re, col_im = get_tiles(up_in, g)
        parts = scatter(*hots, jnp.concatenate([row_im, -row_re], axis=1), -col_im, col_re)
        for a in range(SLOTS):
            total[a * SITES : (a + 1) * SITES, :] += block_of(parts, a)

    own_hots = [scatter_hots(twice(own_index[g])) for g in range(2)]
    for g in range(2):
        if g == 0:
            received_near(reply_in_tiles, 2 * PIECES, 2)
        else:
            received_far(reply_in_tiles, 2 * PIECES, 2, has_lower)
        row_re, row_im, col_re, col_im = get_tiles(reply_in, g)
        shared = jnp.broadcast_to(own[g][:, 1:2], (TILES, LANES))
        turn = jnp.broadcast_to(own[g][:, 2:3], (TILES, LANES))
        parts = scatter(
            *own_hots[g],
            jnp.concatenate(
                [shared * row_re + turn * row_im, shared * row_im - turn * row_re], axis=1
            ),
            shared * col_re - turn * col_im,
            shared * col_im + turn * col_re,
        )
        if g == 0:
            for a in range(SLOTS):
                total[a * SITES : (a + 1) * SITES, :] += block_of(parts, a)
    for a in range(SLOTS):
        value = total[a * SITES : (a + 1) * SITES, :] + block_of(parts, a)
        even_re, odd_re = value[:HALF, :LANES], value[HALF:, :LANES]
        even_im, odd_im = value[:HALF, LANES:], value[HALF:, LANES:]
        even_im = pltpu.roll(even_im, 96, 1)
        odd_re = pltpu.roll(odd_re, 64, 1)
        odd_im = pltpu.roll(odd_im, 32, 1)
        result[pl.ds(a, HALF, stride=24), :] = jnp.where(lane48 < SITES, even_re, even_im)
        result[pl.ds(8 + a, HALF, stride=24), :] = jnp.where(lane48 < 64, even_im, odd_re)
        result[pl.ds(16 + a, HALF, stride=24), :] = jnp.where(lane48 < 32, odd_re, odd_im)
    sent(tag_in_tiles, 1, 0, has_lower)
    sent(up_in_tiles, 2 * PIECES, 1, has_lower)
    sent(reply_in_tiles, 2 * PIECES, 2, has_upper)


def on_device(
    section_state,
    coupling,
    site_energy,
    bath_rate,
    bath_strength,
    bath_of_site,
    quanta,
    send_list,
    dest_slot,
):
    slots, width = section_state.shape
    chunks = width // LANES
    tiled = section_state.reshape(slots, chunks, LANES).transpose(1, 0, 2).reshape(-1, LANES)
    operands = (
        tiled,
        coupling,
        site_energy.reshape(1, SITES),
        bath_rate.reshape(1, SITES),
        bath_strength.reshape(1, SITES),
        bath_of_site.reshape(1, SITES),
        quanta.T,
        send_list,
        dest_slot,
    )
    tile_buffer = pltpu.VMEM((TILES * 8, LANES), F32)
    out = pl.pallas_call(
        kernel,
        out_shape=pltpu.VMEM(tiled.shape, F32),
        in_specs=[pl.BlockSpec(memory_space=pltpu.HBM)] * 9,
        out_specs=pl.BlockSpec(memory_space=pltpu.VMEM),
        scratch_shapes=[
            pltpu.VMEM(tiled.shape, F32),
            pltpu.VMEM((SITES, SITES), F32),
            pltpu.VMEM((3, 1, SITES), F32),
            pltpu.VMEM((1, SITES), jnp.int32),
            pltpu.VMEM((DEPTH, SLOTS), jnp.int32),
            pltpu.VMEM((1, LANES), jnp.int32),
            pltpu.VMEM((1, LANES), jnp.int32),
            tile_buffer,
            tile_buffer,
            tile_buffer,
            tile_buffer,
            tile_buffer,
            tile_buffer,
            pltpu.VMEM((LANES, LANES), F32),
            pltpu.VMEM((LANES, LANES), F32),
            pltpu.VMEM((SLOTS * LANES, 2 * LANES), BF16),
            pltpu.VMEM((SLOTS * LANES, 2 * LANES), BF16),
            pltpu.VMEM((2 * SLOTS * SITES, LANES), F32),
            pltpu.VMEM((SLOTS * SITES, PIECES * LANES), BF16),
            pltpu.VMEM((SLOTS * SITES, PIECES * LANES), BF16),
            pltpu.VMEM((SLOTS * SITES, 2 * LANES), F32),
            pltpu.SemaphoreType.DMA,
            pltpu.SemaphoreType.DMA((8,)),
            pltpu.SemaphoreType.DMA((3,)),
            pltpu.SemaphoreType.DMA((6,)),
        ],
        compiler_params=pltpu.CompilerParams(
            collective_id=0, has_side_effects=True, vmem_limit_bytes=32 * 1024 * 1024
        ),
    )(*[pltpu.with_memory_space_constraint(value, pltpu.HBM) for value in operands])
    return out.reshape(chunks, slots, LANES).transpose(1, 0, 2).reshape(slots, width)


def solution(mesh):
    return jax.shard_map(
        on_device,
        mesh=mesh,
        in_specs=(
            P(("tier", "aux"), None),
            P(),
            P(),
            P(),
            P(),
            P(),
            P(("tier", "aux"), None),
            P(("tier", "aux"), None),
            P(("tier", "aux"), None),
        ),
        out_specs=P(("tier", "aux"), None),
        check_vma=False,
    )
```

```python
import functools

import jax
import jax.numpy as jnp
from jax import lax
from jax.experimental import pallas as pl
from jax.experimental.pallas import tpu as pltpu
from jax.sharding import PartitionSpec as P

MESH = pl.DeviceIdType.MESH
F32 = jnp.float32
BF16 = jnp.bfloat16
SITES = 96
HALF = 48
SLOTS = 8
DEPTH = 4
PIECES = 3
PEERS = 32
TILES = 2 * PEERS
LANES = 128
TIERS = 8


def routes():
    found = [
        (across, dy, dx, dc)
        for across in range(2)
        for dy in range(4)
        for dx in range(4)
        for dc in range(2)
        if (across, dy, dx, dc) != (0, 0, 0, 0)
    ]
    return sorted(found, key=lambda s: (-(s[0] + min(s[1], 4 - s[1]) + min(s[2], 4 - s[2])), -s[3]))


ROUTES = routes()


def split_pair(value):
    high = value.astype(BF16)
    return high, (value - high.astype(F32)).astype(BF16)


def mxu(left, right):
    return jnp.dot(left, right, preferred_element_type=F32)


def kernel(
    state_hbm,
    coupling_hbm,
    energy_hbm,
    rate_hbm,
    strength_hbm,
    bath_hbm,
    quanta_hbm,
    send_hbm,
    dest_hbm,
    result,
    raw,
    coupling_v,
    table_v,
    bath_v,
    quanta_v,
    send_v,
    dest_v,
    tag_out,
    tag_in,
    up_out,
    up_in,
    reply_out,
    reply_in,
    tag_cols,
    own_cols,
    rows_hi,
    rows_lo,
    natural,
    table,
    total,
    load_sem,
    small_sem,
    send_sem,
    recv_sem,
):
    tier = lax.axis_index("tier")
    peer = lax.axis_index("aux")
    my_y = peer // 8
    my_x = lax.rem(peer, 8) // 2
    my_c = lax.rem(peer, 2)

    at_y = [lax.rem(my_y + d, 4) * 8 for d in range(4)]
    at_x = [lax.rem(my_x + d, 4) * 2 for d in range(4)]
    at_c = [my_c, 1 - my_c]

    def partner(dy, dx, dc):
        return at_y[dy % 4] + at_x[dx % 4] + at_c[dc]

    barrier = pltpu.get_barrier_semaphore()

    def greet(up, dy, dx, dc):
        pl.semaphore_signal(
            barrier,
            inc=1,
            device_id=(tier + up, partner(dy, dx, dc)),
            device_id_type=MESH,
        )

    def farthest_first(act, allowed, chosen=(0, 1)):
        if chosen == (0,):
            for hop in ROUTES:
                if not hop[0]:
                    act(*hop)
            return

        @pl.when(allowed)
        def _():
            for hop in ROUTES:
                if hop[0] in chosen:
                    act(*hop)

        if 0 not in chosen:
            return

        @pl.when(jnp.logical_not(allowed))
        def _():
            for hop in ROUTES:
                if not hop[0]:
                    act(*hop)

    has_lower = tier > 0
    has_upper = tier < TIERS - 1
    farthest_first(greet, has_upper)

    small = [
        pltpu.make_async_copy(send_hbm, send_v, small_sem.at[0]),
        pltpu.make_async_copy(dest_hbm, dest_v, small_sem.at[1]),
        pltpu.make_async_copy(quanta_hbm, quanta_v, small_sem.at[2]),
        pltpu.make_async_copy(rate_hbm, table_v.at[0], small_sem.at[3]),
        pltpu.make_async_copy(strength_hbm, table_v.at[1], small_sem.at[4]),
        pltpu.make_async_copy(energy_hbm, table_v.at[2], small_sem.at[5]),
        pltpu.make_async_copy(bath_hbm, bath_v, small_sem.at[6]),
        pltpu.make_async_copy(coupling_hbm, coupling_v, small_sem.at[7]),
    ]
    for copy in small:
        copy.start()
    load = pltpu.make_async_copy(state_hbm, raw, load_sem)
    load.start()
    for copy in small:
        copy.wait()

    lane = lax.broadcasted_iota(jnp.int32, (1, LANES), 1)
    sub8 = lax.broadcasted_iota(jnp.int32, (SLOTS, LANES), 0)
    sub96 = lax.broadcasted_iota(jnp.int32, (SITES, LANES), 0)
    quanta = jnp.concatenate(
        [
            jnp.concatenate([quanta_v[...], jnp.zeros((DEPTH, LANES - SLOTS), jnp.int32)], axis=1),
            jnp.zeros((SLOTS - DEPTH, LANES), jnp.int32),
        ],
        axis=0,
    ).T[:SLOTS]

    def quanta_of(entry):
        slot = entry >> 2
        place = entry & 3
        hit = sub8 == jnp.broadcast_to(slot, (SLOTS, LANES))
        found = [
            jnp.sum(
                jnp.where(hit, jnp.broadcast_to(quanta[:, p : p + 1], (SLOTS, LANES)), 0),
                axis=0,
                keepdims=True,
            )
            for p in range(DEPTH)
        ]
        site = found[3]
        for p in range(DEPTH - 1):
            site = jnp.where(place == p, found[p], site)
        count = sum((found[p] == site).astype(F32) for p in range(DEPTH))
        return slot, site, count

    pad = jnp.zeros((1, LANES - SITES), F32)
    base = jnp.concatenate(
        [
            jnp.concatenate([bath_v[...].astype(F32), pad], axis=1),
            jnp.concatenate([table_v[0], pad], axis=1),
            jnp.concatenate([table_v[1], pad], axis=1),
            jnp.concatenate([table_v[2], pad], axis=1),
            jnp.zeros((LANES - 4, LANES), F32),
        ],
        axis=0,
    ).T
    bath_col = base[:SITES, 0:1]
    rate_col = base[:SITES, 1:2]
    strength_col = base[:SITES, 2:3]
    sub96f = sub96.astype(F32)

    def look_up(site, columns):
        hit = sub96 == jnp.broadcast_to(site, (SITES, LANES))
        bath = jnp.sum(
            jnp.where(hit, jnp.broadcast_to(bath_col, (SITES, LANES)), 0.0), axis=0, keepdims=True
        )
        hit = sub96f == jnp.broadcast_to(bath, (SITES, LANES))
        return [
            jnp.sum(
                jnp.where(hit, jnp.broadcast_to(column, (SITES, LANES)), 0.0), axis=0, keepdims=True
            )
            for column in columns
        ]

    entry = send_v[...]
    slot, site, weight = quanta_of(jnp.maximum(entry, 0))
    group = lane // (LANES // 2)
    usable = (entry >= 0) & (site >= 0) & (tier - group >= 0)
    strength_l, rate_l = look_up(site, [strength_col, rate_col])
    lower = dest_v[...]

    def marked(value):
        return jnp.where(usable, value, -1).astype(F32)

    tag_cols[...] = jnp.broadcast_to(marked(lower * SITES + site), (LANES, LANES)).T
    left_half = lax.broadcasted_iota(jnp.int32, (TILES, LANES), 1) < TILES
    tag_out[pl.ds(0, TILES, stride=8), :] = jnp.where(
        left_half, tag_cols[pl.ds(0, TILES, stride=2), :], tag_cols[pl.ds(1, TILES, stride=2), :]
    )
    tags = jnp.concatenate(
        [
            marked(slot * SITES + site),
            jnp.where(usable, -weight * (strength_l * rate_l), 0.0),
            jnp.where(usable, weight * strength_l, 0.0),
            jnp.zeros((LANES - 3, LANES), F32),
        ],
        axis=0,
    ).T
    own_cols[...] = tags
    own = [
        jnp.concatenate(
            [own_cols[pl.ds(TILES * g + c, PEERS, stride=2), :] for c in range(2)], axis=0
        )
        for g in range(2)
    ]
    tag_tiles = tag_out.reshape(TILES, 8, LANES)
    tag_in_tiles = tag_in.reshape(TILES, 8, LANES)
    up_tiles = up_out.reshape(TILES, 8, LANES)
    up_in_tiles = up_in.reshape(TILES, 8, LANES)
    reply_tiles = reply_out.reshape(TILES, 8, LANES)
    reply_in_tiles = reply_in.reshape(TILES, 8, LANES)

    def exchange(source, target, rows, which, step_tier, allowed, chosen=(0, 1)):
        def send(across, dy, dx, dc):
            q = partner(dy, dx, dc)
            pltpu.make_async_remote_copy(
                source.at[PEERS * across + q, pl.ds(0, rows)],
                target.at[PEERS * across + peer, pl.ds(0, rows)],
                send_sem.at[which],
                recv_sem.at[2 * which + across],
                device_id=(tier + step_tier * across, q),
                device_id_type=MESH,
            ).start()

        farthest_first(send, allowed, chosen)

    def await_near(target, rows, semaphore):
        block = target.at[pl.ds(0, PEERS - 1), pl.ds(0, rows)]
        pltpu.make_async_copy(block, block, semaphore).wait()

    def await_far(target, rows, semaphore, allowed):
        @pl.when(allowed)
        def _():
            block = target.at[pl.ds(0, PEERS), pl.ds(0, rows)]
            pltpu.make_async_copy(block, block, semaphore).wait()

    def received_near(target, rows, which):
        await_near(target, rows, recv_sem.at[2 * which])

    def received_far(target, rows, which, allowed):
        await_far(target, rows, recv_sem.at[2 * which + 1], allowed)

    def sent(target, rows, which, allowed):
        await_near(target, rows, send_sem.at[which])
        await_far(target, rows, send_sem.at[which], allowed)

    self_row = pl.multiple_of(peer * 8, 8)
    tag_in[pl.ds(self_row, 8), :] = tag_out[pl.ds(self_row, 8), :]

    @pl.when(tier == TIERS - 1)
    def _():
        tag_in[PEERS * 8 :, :] = jnp.full((PEERS * 8, LANES), -1.0, F32)
        up_in[PEERS * 8 :, :] = jnp.zeros((PEERS * 8, LANES), F32)

    @pl.when(tier == 0)
    def _():
        reply_in[PEERS * 8 :, :] = jnp.zeros((PEERS * 8, LANES), F32)

    pl.semaphore_wait(barrier, jnp.where(has_lower, 2 * PEERS - 1, PEERS - 1))

    exchange(tag_tiles, tag_in_tiles, 1, 0, -1, has_lower)

    load.wait()
    lane48 = lax.broadcasted_iota(jnp.int32, (HALF, LANES), 1)
    lane96 = lax.broadcasted_iota(jnp.int32, (SITES, LANES), 1)
    zero48 = jnp.zeros((HALF, LANES), F32)
    gap = jnp.zeros((LANES - SITES, LANES), F32)
    ok = lane48 < SITES
    for a in range(SLOTS):
        t0 = raw[pl.ds(a, HALF, stride=24), :]
        t1 = raw[pl.ds(8 + a, HALF, stride=24), :]
        t2 = raw[pl.ds(16 + a, HALF, stride=24), :]
        odd0 = jnp.where(lane48 < 64, pltpu.roll(t1, 64, 1), pltpu.roll(t2, 64, 1))
        odd1 = pltpu.roll(t2, 64, 1)
        left_at, right_at = a * SITES, (SLOTS + a) * SITES
        natural[pl.ds(left_at, HALF, stride=2), :] = t0
        natural[pl.ds(right_at, HALF, stride=2), :] = t1
        natural[pl.ds(left_at + 1, HALF, stride=2), :] = odd0
        natural[pl.ds(right_at + 1, HALF, stride=2), :] = odd1
        even_im = jnp.where(
            lane48 < 32, pltpu.roll(t0, 32, 1), jnp.where(ok, pltpu.roll(t1, 32, 1), zero48)
        )
        odd_im = jnp.where(ok, pltpu.roll(t2, 96, 1), zero48)
        real = jnp.concatenate(
            [jnp.where(ok, t0, zero48), jnp.where(ok, odd0, zero48), gap], axis=0
        )
        imag = jnp.concatenate([even_im, odd_im, gap], axis=0)
        high, low = split_pair(jnp.concatenate([real, imag], axis=1))
        block = slice(a * LANES, (a + 1) * LANES)
        rows_hi[block, :] = high
        rows_lo[block, :] = low
        turned_re = pltpu.roll(real.T[:SITES], 64, 1)
        turned_im = pltpu.roll(imag.T[:SITES], 32, 1)
        block = slice(a * SITES, (a + 1) * SITES)
        high, low = split_pair(
            jnp.concatenate(
                [
                    natural[left_at : left_at + SITES, :],
                    jnp.where(
                        lane96 < 64, natural[right_at : right_at + SITES, :], turned_re
                    ),
                    jnp.where(lane96 < 32, turned_re, turned_im),
                ],
                axis=1,
            )
        )
        table[block, :] = jnp.concatenate([high, low], axis=1)

    lane_f = lax.broadcasted_iota(jnp.int32, (LANES, LANES), 1).astype(F32)

    def one_hot(index, chunks):
        return jnp.concatenate(
            [
                jnp.where(lane_f[: index.shape[0]] == index - float(LANES * k), 1.0, 0.0).astype(BF16)
                for k in range(chunks)
            ],
            axis=1,
        )

    def gather(index):
        hot = one_hot(index, SLOTS * SITES // LANES)
        found = mxu(hot, table[...])
        return found[:, : PIECES * LANES] + found[:, PIECES * LANES :]

    def put_tiles(target, g, packed):
        for c in range(2):
            for k in range(PIECES):
                target[pl.ds(PEERS * 8 * g + PIECES * c + k, PEERS, stride=8), :] = packed[
                    c * PEERS : (c + 1) * PEERS, k * LANES : (k + 1) * LANES
                ]

    lane_h = lane_f[: 2 * PEERS]

    def get_tiles(source, g):
        def piece(k):
            return jnp.concatenate(
                [
                    source[pl.ds(PEERS * 8 * g + PIECES * c + k, PEERS, stride=8), :]
                    for c in range(2)
                ],
                axis=0,
            )

        first, middle, last = piece(0), piece(1), piece(2)
        row_im = jnp.where(lane_h < 32.0, pltpu.roll(first, 32, 1), pltpu.roll(middle, 32, 1))
        col_re = jnp.where(lane_h < 64.0, pltpu.roll(middle, 64, 1), pltpu.roll(last, 64, 1))
        return first, row_im, col_re, pltpu.roll(last, 96, 1)

    own_index = [jnp.broadcast_to(own[g][:, 0:1], (TILES, LANES)) for g in range(2)]
    packed = gather(jnp.concatenate(own_index, axis=0))
    for g in range(2):
        put_tiles(up_out, g, packed[g * TILES : (g + 1) * TILES])
    up_in[pl.ds(self_row, 8), :] = up_out[pl.ds(self_row, 8), :]
    exchange(up_tiles, up_in_tiles, 2 * PIECES, 1, -1, has_lower)

    asked = []
    for g in range(2):
        if g == 0:
            received_near(tag_in_tiles, 1, 0)
        else:
            received_far(tag_in_tiles, 1, 0, has_upper)
        both = tag_in[pl.ds(PEERS * 8 * g, PEERS, stride=8), :]
        swapped = pltpu.roll(both, TILES, 1)
        index = jnp.concatenate(
            [
                jnp.where(left_half[:PEERS], both, swapped),
                jnp.where(left_half[:PEERS], swapped, both),
            ],
            axis=0,
        )
        asked.append(index)
        put_tiles(reply_out, g, gather(index))
        exchange(reply_tiles, reply_in_tiles, 2 * PIECES, 2, 1, has_upper if g else True, (g,))
    reply_in[pl.ds(self_row, 8), :] = reply_out[pl.ds(self_row, 8), :]

    diagonal = lax.broadcasted_iota(jnp.int32, (SITES, SITES), 0) == lax.broadcasted_iota(
        jnp.int32, (SITES, SITES), 1
    )
    coupling = coupling_v[...]
    hamilton = (coupling + coupling.T) * 0.5 + jnp.where(
        diagonal, jnp.broadcast_to(base[:SITES, 3:4], (SITES, SITES)), 0.0
    )
    row_id = lax.broadcasted_iota(jnp.int32, (SITES, SITES), 0)
    site_of_row = jnp.where(row_id < HALF, 2 * row_id, 2 * (row_id - HALF) + 1)
    chooser = jnp.where(
        site_of_row == lax.broadcasted_iota(jnp.int32, (SITES, SITES), 1), 1.0, 0.0
    ).astype(BF16)
    h_hi, h_lo = split_pair(hamilton)
    p_hi = mxu(chooser, h_hi).astype(BF16)
    p_lo = mxu(chooser, h_lo).astype(BF16)
    p_hi = mxu(p_hi, chooser.T).astype(BF16)
    p_lo = mxu(p_lo, chooser.T).astype(BF16)
    gap_r = jnp.zeros((SITES, LANES - SITES), BF16)
    left_hi = jnp.concatenate([p_hi, gap_r], axis=1)
    left_lo = jnp.concatenate([p_lo, gap_r], axis=1)
    gap_b = jnp.zeros((LANES - SITES, LANES), BF16)

    def turned_pair(h):
        square = jnp.concatenate([jnp.concatenate([h, gap_r], axis=1), gap_b], axis=0)
        empty = jnp.zeros((LANES, LANES), BF16)
        return jnp.concatenate(
            [
                jnp.concatenate([empty, square], axis=1),
                jnp.concatenate([-square, empty], axis=1),
            ],
            axis=0,
        )

    right_hi = turned_pair(h_hi)
    right_lo = turned_pair(h_lo)

    edge_slot, edge_site, _ = quanta_of(jnp.minimum(lane, SLOTS * DEPTH - 1))
    (edge_rate,) = look_up(edge_site, [rate_col])
    edge_rate = jnp.where((lane < SLOTS * DEPTH) & (edge_site >= 0), edge_rate, 0.0)
    damping = jnp.sum(
        jnp.where(
            sub8 == jnp.broadcast_to(edge_slot, (SLOTS, LANES)),
            jnp.broadcast_to(edge_rate, (SLOTS, LANES)),
            0.0,
        ),
        axis=1,
        keepdims=True,
    )

    for a in range(SLOTS):
        z_hi = rows_hi[a * LANES : (a + 1) * LANES, :]
        z_lo = rows_lo[a * LANES : (a + 1) * LANES, :]
        left = mxu(left_hi, z_hi) + mxu(left_hi, z_lo) + mxu(left_lo, z_hi)
        z_hi = z_hi[:SITES]
        z_lo = z_lo[:SITES]
        right = mxu(z_hi, right_hi) + mxu(z_lo, right_hi) + mxu(z_hi, right_lo)
        z = z_hi.astype(F32) + z_lo.astype(F32)
        total[a * SITES : (a + 1) * SITES, :] = (
            jnp.concatenate([left[:, LANES:], -left[:, :LANES]], axis=1)
            + right
            - damping[a : a + 1, 0:1] * z
        )

    sub768 = lax.broadcasted_iota(jnp.int32, (SLOTS * SITES, LANES), 0).astype(F32)

    def scatter_hots(index):
        slot_f = jnp.floor((index + 0.5) * (1.0 / SITES))
        site_f = index - float(SITES) * slot_f
        half = jnp.floor(site_f * 0.5)
        in_order = float(SITES) * slot_f + half + float(HALF) * (site_f - 2.0 * half)
        row_hot = jnp.where(
            sub768 == jnp.broadcast_to(in_order.T[0:1], (SLOTS * SITES, LANES)), 1.0, 0.0
        ).astype(BF16)
        col_hot = one_hot(float(LANES) * slot_f + site_f, SLOTS)
        return row_hot, col_hot

    def scatter(row_hots, col_hots, row_data, col_re, col_im):
        high, low = split_pair(row_data)
        by_row = mxu(row_hots, jnp.concatenate([high, low], axis=0))
        turned = []
        for column in (col_re, col_im):
            high, low = split_pair(column)
            stacked = jnp.concatenate([high.astype(F32), low.astype(F32)], axis=0)
            turned.append(stacked.T[:SITES].astype(BF16))
        by_col = mxu(jnp.concatenate(turned, axis=0), col_hots)
        return by_row, by_col

    def block_of(parts, a):
        by_row, by_col = parts
        lanes = slice(a * LANES, (a + 1) * LANES)
        return by_row[a * SITES : (a + 1) * SITES] + jnp.concatenate(
            [by_col[:SITES, lanes], by_col[SITES:, lanes]], axis=1
        )

    def twice(index):
        return jnp.concatenate([index, index], axis=0)

    for g in range(2):
        hots = scatter_hots(twice(asked[g]))
        if g == 0:
            received_near(up_in_tiles, 2 * PIECES, 1)
        else:
            received_far(up_in_tiles, 2 * PIECES, 1, has_upper)
        row_re, row_im, col_re, col_im = get_tiles(up_in, g)
        parts = scatter(*hots, jnp.concatenate([row_im, -row_re], axis=1), -col_im, col_re)
        for a in range(SLOTS):
            total[a * SITES : (a + 1) * SITES, :] += block_of(parts, a)

    own_hots = [scatter_hots(twice(own_index[g])) for g in range(2)]
    for g in range(2):
        if g == 0:
            received_near(reply_in_tiles, 2 * PIECES, 2)
        else:
            received_far(reply_in_tiles, 2 * PIECES, 2, has_lower)
        row_re, row_im, col_re, col_im = get_tiles(reply_in, g)
        shared = jnp.broadcast_to(own[g][:, 1:2], (TILES, LANES))
        turn = jnp.broadcast_to(own[g][:, 2:3], (TILES, LANES))
        parts = scatter(
            *own_hots[g],
            jnp.concatenate(
                [shared * row_re + turn * row_im, shared * row_im - turn * row_re], axis=1
            ),
            shared * col_re - turn * col_im,
            shared * col_im + turn * col_re,
        )
        if g == 0:
            for a in range(SLOTS):
                total[a * SITES : (a + 1) * SITES, :] += block_of(parts, a)
    for a in range(SLOTS):
        value = total[a * SITES : (a + 1) * SITES, :] + block_of(parts, a)
        even_re, odd_re = value[:HALF, :LANES], value[HALF:, :LANES]
        even_im, odd_im = value[:HALF, LANES:], value[HALF:, LANES:]
        even_im = pltpu.roll(even_im, 96, 1)
        odd_re = pltpu.roll(odd_re, 64, 1)
        odd_im = pltpu.roll(odd_im, 32, 1)
        result[pl.ds(a, HALF, stride=24), :] = jnp.where(lane48 < SITES, even_re, even_im)
        result[pl.ds(8 + a, HALF, stride=24), :] = jnp.where(lane48 < 64, even_im, odd_re)
        result[pl.ds(16 + a, HALF, stride=24), :] = jnp.where(lane48 < 32, odd_re, odd_im)
    sent(tag_in_tiles, 1, 0, has_lower)
    sent(up_in_tiles, 2 * PIECES, 1, has_lower)
    sent(reply_in_tiles, 2 * PIECES, 2, has_upper)


def on_device(
    section_state,
    coupling,
    site_energy,
    bath_rate,
    bath_strength,
    bath_of_site,
    quanta,
    send_list,
    dest_slot,
):
    slots, width = section_state.shape
    chunks = width // LANES
    tiled = section_state.reshape(slots, chunks, LANES).transpose(1, 0, 2).reshape(-1, LANES)
    operands = (
        tiled,
        coupling,
        site_energy.reshape(1, SITES),
        bath_rate.reshape(1, SITES),
        bath_strength.reshape(1, SITES),
        bath_of_site.reshape(1, SITES),
        quanta.T,
        send_list,
        dest_slot,
    )
    tile_buffer = pltpu.VMEM((TILES * 8, LANES), F32)
    out = pl.pallas_call(
        kernel,
        out_shape=pltpu.VMEM(tiled.shape, F32),
        in_specs=[pl.BlockSpec(memory_space=pltpu.HBM)] * 9,
        out_specs=pl.BlockSpec(memory_space=pltpu.VMEM),
        scratch_shapes=[
            pltpu.VMEM(tiled.shape, F32),
            pltpu.VMEM((SITES, SITES), F32),
            pltpu.VMEM((3, 1, SITES), F32),
            pltpu.VMEM((1, SITES), jnp.int32),
            pltpu.VMEM((DEPTH, SLOTS), jnp.int32),
            pltpu.VMEM((1, LANES), jnp.int32),
            pltpu.VMEM((1, LANES), jnp.int32),
            tile_buffer,
            tile_buffer,
            tile_buffer,
            tile_buffer,
            tile_buffer,
            tile_buffer,
            pltpu.VMEM((LANES, LANES), F32),
            pltpu.VMEM((LANES, LANES), F32),
            pltpu.VMEM((SLOTS * LANES, 2 * LANES), BF16),
            pltpu.VMEM((SLOTS * LANES, 2 * LANES), BF16),
            pltpu.VMEM((2 * SLOTS * SITES, LANES), F32),
            pltpu.VMEM((SLOTS * SITES, 2 * PIECES * LANES), BF16),
            pltpu.VMEM((SLOTS * SITES, 2 * LANES), F32),
            pltpu.SemaphoreType.DMA,
            pltpu.SemaphoreType.DMA((8,)),
            pltpu.SemaphoreType.DMA((3,)),
            pltpu.SemaphoreType.DMA((6,)),
        ],
        compiler_params=pltpu.CompilerParams(
            collective_id=0, has_side_effects=True, vmem_limit_bytes=32 * 1024 * 1024
        ),
    )(*[pltpu.with_memory_space_constraint(value, pltpu.HBM) for value in operands])
    return out.reshape(chunks, slots, LANES).transpose(1, 0, 2).reshape(slots, width)


def solution(mesh):
    return jax.shard_map(
        on_device,
        mesh=mesh,
        in_specs=(
            P(("tier", "aux"), None),
            P(),
            P(),
            P(),
            P(),
            P(),
            P(("tier", "aux"), None),
            P(("tier", "aux"), None),
            P(("tier", "aux"), None),
        ),
        out_specs=P(("tier", "aux"), None),
        check_vma=False,
    )
```

```python
import functools

import jax
import jax.numpy as jnp
from jax import lax
from jax.experimental import pallas as pl
from jax.experimental.pallas import tpu as pltpu
from jax.sharding import PartitionSpec as P

MESH = pl.DeviceIdType.MESH
F32 = jnp.float32
BF16 = jnp.bfloat16
SITES = 96
HALF = 48
SLOTS = 8
DEPTH = 4
PIECES = 3
PEERS = 32
TILES = 2 * PEERS
LANES = 128
TIERS = 8


def routes():
    found = [
        (across, dy, dx, dc)
        for across in range(2)
        for dy in range(4)
        for dx in range(4)
        for dc in range(2)
        if (across, dy, dx, dc) != (0, 0, 0, 0)
    ]
    return sorted(found, key=lambda s: (-(s[0] + min(s[1], 4 - s[1]) + min(s[2], 4 - s[2])), -s[3]))


ROUTES = routes()


def split_pair(value):
    high = value.astype(BF16)
    return high, (value - high.astype(F32)).astype(BF16)


def mxu(left, right):
    return jnp.dot(left, right, preferred_element_type=F32)


def kernel(
    state_hbm,
    coupling_hbm,
    energy_hbm,
    rate_hbm,
    strength_hbm,
    bath_hbm,
    quanta_hbm,
    send_hbm,
    dest_hbm,
    result,
    raw,
    coupling_v,
    table_v,
    bath_v,
    quanta_v,
    send_v,
    dest_v,
    tag_out,
    tag_in,
    up_out,
    up_in,
    reply_out,
    reply_in,
    tag_cols,
    own_cols,
    rows_hi,
    rows_lo,
    natural,
    table,
    total,
    load_sem,
    small_sem,
    send_sem,
    recv_sem,
):
    tier = lax.axis_index("tier")
    peer = lax.axis_index("aux")
    my_y = peer // 8
    my_x = lax.rem(peer, 8) // 2
    my_c = lax.rem(peer, 2)

    at_y = [lax.rem(my_y + d, 4) * 8 for d in range(4)]
    at_x = [lax.rem(my_x + d, 4) * 2 for d in range(4)]
    at_c = [my_c, 1 - my_c]

    def partner(dy, dx, dc):
        return at_y[dy % 4] + at_x[dx % 4] + at_c[dc]

    barrier = pltpu.get_barrier_semaphore()

    def greet(up, dy, dx, dc):
        pl.semaphore_signal(
            barrier,
            inc=1,
            device_id=(tier + up, partner(dy, dx, dc)),
            device_id_type=MESH,
        )

    def farthest_first(act, allowed, chosen=(0, 1)):
        if chosen == (0,):
            for hop in ROUTES:
                if not hop[0]:
                    act(*hop)
            return

        @pl.when(allowed)
        def _():
            for hop in ROUTES:
                if hop[0] in chosen:
                    act(*hop)

        if 0 not in chosen:
            return

        @pl.when(jnp.logical_not(allowed))
        def _():
            for hop in ROUTES:
                if not hop[0]:
                    act(*hop)

    has_lower = tier > 0
    has_upper = tier < TIERS - 1
    farthest_first(greet, has_upper)

    small = [
        pltpu.make_async_copy(send_hbm, send_v, small_sem.at[0]),
        pltpu.make_async_copy(dest_hbm, dest_v, small_sem.at[1]),
        pltpu.make_async_copy(quanta_hbm, quanta_v, small_sem.at[2]),
        pltpu.make_async_copy(rate_hbm, table_v.at[0], small_sem.at[3]),
        pltpu.make_async_copy(strength_hbm, table_v.at[1], small_sem.at[4]),
        pltpu.make_async_copy(energy_hbm, table_v.at[2], small_sem.at[5]),
        pltpu.make_async_copy(bath_hbm, bath_v, small_sem.at[6]),
        pltpu.make_async_copy(coupling_hbm, coupling_v, small_sem.at[7]),
    ]
    for copy in small:
        copy.start()
    load = pltpu.make_async_copy(state_hbm, raw, load_sem)
    load.start()
    for copy in small:
        copy.wait()

    lane = lax.broadcasted_iota(jnp.int32, (1, LANES), 1)
    sub8 = lax.broadcasted_iota(jnp.int32, (SLOTS, LANES), 0)
    sub96 = lax.broadcasted_iota(jnp.int32, (SITES, LANES), 0)
    quanta = jnp.concatenate(
        [
            jnp.concatenate([quanta_v[...], jnp.zeros((DEPTH, LANES - SLOTS), jnp.int32)], axis=1),
            jnp.zeros((SLOTS - DEPTH, LANES), jnp.int32),
        ],
        axis=0,
    ).T[:SLOTS]

    def quanta_of(entry):
        slot = entry >> 2
        place = entry & 3
        hit = sub8 == jnp.broadcast_to(slot, (SLOTS, LANES))
        found = [
            jnp.sum(
                jnp.where(hit, jnp.broadcast_to(quanta[:, p : p + 1], (SLOTS, LANES)), 0),
                axis=0,
                keepdims=True,
            )
            for p in range(DEPTH)
        ]
        site = found[3]
        for p in range(DEPTH - 1):
            site = jnp.where(place == p, found[p], site)
        count = sum((found[p] == site).astype(F32) for p in range(DEPTH))
        return slot, site, count

    pad = jnp.zeros((1, LANES - SITES), F32)
    base = jnp.concatenate(
        [
            jnp.concatenate([bath_v[...].astype(F32), pad], axis=1),
            jnp.concatenate([table_v[0], pad], axis=1),
            jnp.concatenate([table_v[1], pad], axis=1),
            jnp.concatenate([table_v[2], pad], axis=1),
            jnp.zeros((LANES - 4, LANES), F32),
        ],
        axis=0,
    ).T
    bath_col = base[:SITES, 0:1]
    rate_col = base[:SITES, 1:2]
    strength_col = base[:SITES, 2:3]
    sub96f = sub96.astype(F32)

    def look_up(site, columns):
        hit = sub96 == jnp.broadcast_to(site, (SITES, LANES))
        bath = jnp.sum(
            jnp.where(hit, jnp.broadcast_to(bath_col, (SITES, LANES)), 0.0), axis=0, keepdims=True
        )
        hit = sub96f == jnp.broadcast_to(bath, (SITES, LANES))
        return [
            jnp.sum(
                jnp.where(hit, jnp.broadcast_to(column, (SITES, LANES)), 0.0), axis=0, keepdims=True
            )
            for column in columns
        ]

    entry = send_v[...]
    slot, site, weight = quanta_of(jnp.maximum(entry, 0))
    group = lane // (LANES // 2)
    usable = (entry >= 0) & (site >= 0) & (tier - group >= 0)
    strength_l, rate_l = look_up(site, [strength_col, rate_col])
    lower = dest_v[...]

    def marked(value):
        return jnp.where(usable, value, -1).astype(F32)

    tag_cols[...] = jnp.broadcast_to(marked(lower * SITES + site), (LANES, LANES)).T
    left_half = lax.broadcasted_iota(jnp.int32, (TILES, LANES), 1) < TILES
    tag_out[pl.ds(0, TILES, stride=8), :] = jnp.where(
        left_half, tag_cols[pl.ds(0, TILES, stride=2), :], tag_cols[pl.ds(1, TILES, stride=2), :]
    )
    tags = jnp.concatenate(
        [
            marked(slot * SITES + site),
            jnp.where(usable, -weight * (strength_l * rate_l), 0.0),
            jnp.where(usable, weight * strength_l, 0.0),
            jnp.zeros((LANES - 3, LANES), F32),
        ],
        axis=0,
    ).T
    own_cols[...] = tags
    own = [
        jnp.concatenate(
            [own_cols[pl.ds(TILES * g + c, PEERS, stride=2), :] for c in range(2)], axis=0
        )
        for g in range(2)
    ]
    tag_tiles = tag_out.reshape(TILES, 8, LANES)
    tag_in_tiles = tag_in.reshape(TILES, 8, LANES)
    up_tiles = up_out.reshape(TILES, 8, LANES)
    up_in_tiles = up_in.reshape(TILES, 8, LANES)
    reply_tiles = reply_out.reshape(TILES, 8, LANES)
    reply_in_tiles = reply_in.reshape(TILES, 8, LANES)

    def exchange(source, target, rows, which, step_tier, allowed, chosen=(0, 1)):
        def send(across, dy, dx, dc):
            q = partner(dy, dx, dc)
            pltpu.make_async_remote_copy(
                source.at[PEERS * across + q, pl.ds(0, rows)],
                target.at[PEERS * across + peer, pl.ds(0, rows)],
                send_sem.at[which],
                recv_sem.at[2 * which + across],
                device_id=(tier + step_tier * across, q),
                device_id_type=MESH,
            ).start()

        farthest_first(send, allowed, chosen)

    def await_near(target, rows, semaphore):
        block = target.at[pl.ds(0, PEERS - 1), pl.ds(0, rows)]
        pltpu.make_async_copy(block, block, semaphore).wait()

    def await_far(target, rows, semaphore, allowed):
        @pl.when(allowed)
        def _():
            block = target.at[pl.ds(0, PEERS), pl.ds(0, rows)]
            pltpu.make_async_copy(block, block, semaphore).wait()

    def received_near(target, rows, which):
        await_near(target, rows, recv_sem.at[2 * which])

    def received_far(target, rows, which, allowed):
        await_far(target, rows, recv_sem.at[2 * which + 1], allowed)

    def sent(target, rows, which, allowed):
        await_near(target, rows, send_sem.at[which])
        await_far(target, rows, send_sem.at[which], allowed)

    self_row = pl.multiple_of(peer * 8, 8)
    tag_in[pl.ds(self_row, 8), :] = tag_out[pl.ds(self_row, 8), :]

    @pl.when(tier == TIERS - 1)
    def _():
        tag_in[PEERS * 8 :, :] = jnp.full((PEERS * 8, LANES), -1.0, F32)
        up_in[PEERS * 8 :, :] = jnp.zeros((PEERS * 8, LANES), F32)

    @pl.when(tier == 0)
    def _():
        reply_in[PEERS * 8 :, :] = jnp.zeros((PEERS * 8, LANES), F32)

    pl.semaphore_wait(barrier, jnp.where(has_lower, 2 * PEERS - 1, PEERS - 1))

    exchange(tag_tiles, tag_in_tiles, 1, 0, -1, has_lower)

    load.wait()
    lane48 = lax.broadcasted_iota(jnp.int32, (HALF, LANES), 1)
    lane96 = lax.broadcasted_iota(jnp.int32, (SITES, LANES), 1)
    zero48 = jnp.zeros((HALF, LANES), F32)
    gap = jnp.zeros((LANES - SITES, LANES), F32)
    ok = lane48 < SITES
    for a in range(SLOTS):
        t0 = raw[pl.ds(a, HALF, stride=24), :]
        t1 = raw[pl.ds(8 + a, HALF, stride=24), :]
        t2 = raw[pl.ds(16 + a, HALF, stride=24), :]
        odd0 = jnp.where(lane48 < 64, pltpu.roll(t1, 64, 1), pltpu.roll(t2, 64, 1))
        odd1 = pltpu.roll(t2, 64, 1)
        left_at, right_at = a * SITES, (SLOTS + a) * SITES
        natural[pl.ds(left_at, HALF, stride=2), :] = t0
        natural[pl.ds(right_at, HALF, stride=2), :] = t1
        natural[pl.ds(left_at + 1, HALF, stride=2), :] = odd0
        natural[pl.ds(right_at + 1, HALF, stride=2), :] = odd1
        even_im = jnp.where(
            lane48 < 32, pltpu.roll(t0, 32, 1), jnp.where(ok, pltpu.roll(t1, 32, 1), zero48)
        )
        odd_im = jnp.where(ok, pltpu.roll(t2, 96, 1), zero48)
        real = jnp.concatenate(
            [jnp.where(ok, t0, zero48), jnp.where(ok, odd0, zero48), gap], axis=0
        )
        imag = jnp.concatenate([even_im, odd_im, gap], axis=0)
        high, low = split_pair(jnp.concatenate([real, imag], axis=1))
        block = slice(a * LANES, (a + 1) * LANES)
        rows_hi[block, :] = high
        rows_lo[block, :] = low
        turned_re = pltpu.roll(real.T[:SITES], 64, 1)
        turned_im = pltpu.roll(imag.T[:SITES], 32, 1)
        block = slice(a * SITES, (a + 1) * SITES)
        high, low = split_pair(
            jnp.concatenate(
                [
                    natural[left_at : left_at + SITES, :],
                    jnp.where(
                        lane96 < 64, natural[right_at : right_at + SITES, :], turned_re
                    ),
                    jnp.where(lane96 < 32, turned_re, turned_im),
                ],
                axis=1,
            )
        )
        table[block, :] = jnp.concatenate([high, low], axis=1)

    lane_f = lax.broadcasted_iota(jnp.int32, (LANES, LANES), 1).astype(F32)

    def one_hot(index, chunks):
        return jnp.concatenate(
            [
                jnp.where(lane_f[: index.shape[0]] == index - float(LANES * k), 1.0, 0.0).astype(BF16)
                for k in range(chunks)
            ],
            axis=1,
        )

    def gather(index):
        hot = one_hot(index, SLOTS * SITES // LANES)
        found = mxu(hot, table[...])
        return found[:, : PIECES * LANES] + found[:, PIECES * LANES :]

    def put_tiles(target, g, packed):
        for c in range(2):
            for k in range(PIECES):
                target[pl.ds(PEERS * 8 * g + PIECES * c + k, PEERS, stride=8), :] = packed[
                    c * PEERS : (c + 1) * PEERS, k * LANES : (k + 1) * LANES
                ]

    lane_h = lane_f[: 2 * PEERS]

    def get_tiles(source, g):
        def piece(k):
            return jnp.concatenate(
                [
                    source[pl.ds(PEERS * 8 * g + PIECES * c + k, PEERS, stride=8), :]
                    for c in range(2)
                ],
                axis=0,
            )

        first, middle, last = piece(0), piece(1), piece(2)
        row_im = jnp.where(lane_h < 32.0, pltpu.roll(first, 32, 1), pltpu.roll(middle, 32, 1))
        col_re = jnp.where(lane_h < 64.0, pltpu.roll(middle, 64, 1), pltpu.roll(last, 64, 1))
        return first, row_im, col_re, pltpu.roll(last, 96, 1)

    own_index = [jnp.broadcast_to(own[g][:, 0:1], (TILES, LANES)) for g in range(2)]
    packed = gather(jnp.concatenate(own_index, axis=0))
    for g in range(2):
        put_tiles(up_out, g, packed[g * TILES : (g + 1) * TILES])
    up_in[pl.ds(self_row, 8), :] = up_out[pl.ds(self_row, 8), :]
    exchange(up_tiles, up_in_tiles, 2 * PIECES, 1, -1, has_lower)

    def asked_of(g):
        both = tag_in[pl.ds(PEERS * 8 * g, PEERS, stride=8), :]
        swapped = pltpu.roll(both, TILES, 1)
        return jnp.concatenate(
            [
                jnp.where(left_half[:PEERS], both, swapped),
                jnp.where(left_half[:PEERS], swapped, both),
            ],
            axis=0,
        )

    def answer(g):
        put_tiles(reply_out, g, gather(asked_of(g)))
        for across, dy, dx, dc in ROUTES:
            if across == g:
                q = partner(dy, dx, dc)
                pltpu.make_async_remote_copy(
                    reply_tiles.at[PEERS * g + q, pl.ds(0, 2 * PIECES)],
                    reply_in_tiles.at[PEERS * g + peer, pl.ds(0, 2 * PIECES)],
                    send_sem.at[2],
                    recv_sem.at[4 + g],
                    device_id=(tier + g, q),
                    device_id_type=MESH,
                ).start()

    received_near(tag_in_tiles, 1, 0)
    answer(0)

    @pl.when(has_upper)
    def _():
        block = tag_in_tiles.at[pl.ds(0, PEERS), pl.ds(0, 1)]
        pltpu.make_async_copy(block, block, recv_sem.at[1]).wait()
        answer(1)

    asked = [asked_of(g) for g in range(2)]
    reply_in[pl.ds(self_row, 8), :] = reply_out[pl.ds(self_row, 8), :]

    diagonal = lax.broadcasted_iota(jnp.int32, (SITES, SITES), 0) == lax.broadcasted_iota(
        jnp.int32, (SITES, SITES), 1
    )
    coupling = coupling_v[...]
    hamilton = (coupling + coupling.T) * 0.5 + jnp.where(
        diagonal, jnp.broadcast_to(base[:SITES, 3:4], (SITES, SITES)), 0.0
    )
    row_id = lax.broadcasted_iota(jnp.int32, (SITES, SITES), 0)
    site_of_row = jnp.where(row_id < HALF, 2 * row_id, 2 * (row_id - HALF) + 1)
    chooser = jnp.where(
        site_of_row == lax.broadcasted_iota(jnp.int32, (SITES, SITES), 1), 1.0, 0.0
    ).astype(BF16)
    h_hi, h_lo = split_pair(hamilton)
    p_hi = mxu(chooser, h_hi).astype(BF16)
    p_lo = mxu(chooser, h_lo).astype(BF16)
    p_hi = mxu(p_hi, chooser.T).astype(BF16)
    p_lo = mxu(p_lo, chooser.T).astype(BF16)
    gap_r = jnp.zeros((SITES, LANES - SITES), BF16)
    left_hi = jnp.concatenate([p_hi, gap_r], axis=1)
    left_lo = jnp.concatenate([p_lo, gap_r], axis=1)
    gap_b = jnp.zeros((LANES - SITES, LANES), BF16)

    def turned_pair(h):
        square = jnp.concatenate([jnp.concatenate([h, gap_r], axis=1), gap_b], axis=0)
        empty = jnp.zeros((LANES, LANES), BF16)
        return jnp.concatenate(
            [
                jnp.concatenate([empty, square], axis=1),
                jnp.concatenate([-square, empty], axis=1),
            ],
            axis=0,
        )

    right_hi = turned_pair(h_hi)
    right_lo = turned_pair(h_lo)

    edge_slot, edge_site, _ = quanta_of(jnp.minimum(lane, SLOTS * DEPTH - 1))
    (edge_rate,) = look_up(edge_site, [rate_col])
    edge_rate = jnp.where((lane < SLOTS * DEPTH) & (edge_site >= 0), edge_rate, 0.0)
    damping = jnp.sum(
        jnp.where(
            sub8 == jnp.broadcast_to(edge_slot, (SLOTS, LANES)),
            jnp.broadcast_to(edge_rate, (SLOTS, LANES)),
            0.0,
        ),
        axis=1,
        keepdims=True,
    )

    for a in range(SLOTS):
        z_hi = rows_hi[a * LANES : (a + 1) * LANES, :]
        z_lo = rows_lo[a * LANES : (a + 1) * LANES, :]
        left = mxu(left_hi, z_hi) + mxu(left_hi, z_lo) + mxu(left_lo, z_hi)
        z_hi = z_hi[:SITES]
        z_lo = z_lo[:SITES]
        right = mxu(z_hi, right_hi) + mxu(z_lo, right_hi) + mxu(z_hi, right_lo)
        z = z_hi.astype(F32) + z_lo.astype(F32)
        total[a * SITES : (a + 1) * SITES, :] = (
            jnp.concatenate([left[:, LANES:], -left[:, :LANES]], axis=1)
            + right
            - damping[a : a + 1, 0:1] * z
        )

    sub768 = lax.broadcasted_iota(jnp.int32, (SLOTS * SITES, LANES), 0).astype(F32)

    def scatter_hots(index):
        slot_f = jnp.floor((index + 0.5) * (1.0 / SITES))
        site_f = index - float(SITES) * slot_f
        half = jnp.floor(site_f * 0.5)
        in_order = float(SITES) * slot_f + half + float(HALF) * (site_f - 2.0 * half)
        row_hot = jnp.where(
            sub768 == jnp.broadcast_to(in_order.T[0:1], (SLOTS * SITES, LANES)), 1.0, 0.0
        ).astype(BF16)
        col_hot = one_hot(float(LANES) * slot_f + site_f, SLOTS)
        return row_hot, col_hot

    def scatter(row_hots, col_hots, row_data, col_re, col_im):
        high, low = split_pair(row_data)
        by_row = mxu(row_hots, jnp.concatenate([high, low], axis=0))
        turned = []
        for column in (col_re, col_im):
            high, low = split_pair(column)
            stacked = jnp.concatenate([high.astype(F32), low.astype(F32)], axis=0)
            turned.append(stacked.T[:SITES].astype(BF16))
        by_col = mxu(jnp.concatenate(turned, axis=0), col_hots)
        return by_row, by_col

    def block_of(parts, a):
        by_row, by_col = parts
        lanes = slice(a * LANES, (a + 1) * LANES)
        return by_row[a * SITES : (a + 1) * SITES] + jnp.concatenate(
            [by_col[:SITES, lanes], by_col[SITES:, lanes]], axis=1
        )

    def twice(index):
        return jnp.concatenate([index, index], axis=0)

    for g in range(2):
        hots = scatter_hots(twice(asked[g]))
        if g == 0:
            received_near(up_in_tiles, 2 * PIECES, 1)
        else:
            received_far(up_in_tiles, 2 * PIECES, 1, has_upper)
        row_re, row_im, col_re, col_im = get_tiles(up_in, g)
        parts = scatter(*hots, jnp.concatenate([row_im, -row_re], axis=1), -col_im, col_re)
        for a in range(SLOTS):
            total[a * SITES : (a + 1) * SITES, :] += block_of(parts, a)

    own_hots = [scatter_hots(twice(own_index[g])) for g in range(2)]
    for g in range(2):
        if g == 0:
            received_near(reply_in_tiles, 2 * PIECES, 2)
        else:
            received_far(reply_in_tiles, 2 * PIECES, 2, has_lower)
        row_re, row_im, col_re, col_im = get_tiles(reply_in, g)
        shared = jnp.broadcast_to(own[g][:, 1:2], (TILES, LANES))
        turn = jnp.broadcast_to(own[g][:, 2:3], (TILES, LANES))
        parts = scatter(
            *own_hots[g],
            jnp.concatenate(
                [shared * row_re + turn * row_im, shared * row_im - turn * row_re], axis=1
            ),
            shared * col_re - turn * col_im,
            shared * col_im + turn * col_re,
        )
        if g == 0:
            for a in range(SLOTS):
                total[a * SITES : (a + 1) * SITES, :] += block_of(parts, a)
    for a in range(SLOTS):
        value = total[a * SITES : (a + 1) * SITES, :] + block_of(parts, a)
        even_re, odd_re = value[:HALF, :LANES], value[HALF:, :LANES]
        even_im, odd_im = value[:HALF, LANES:], value[HALF:, LANES:]
        even_im = pltpu.roll(even_im, 96, 1)
        odd_re = pltpu.roll(odd_re, 64, 1)
        odd_im = pltpu.roll(odd_im, 32, 1)
        result[pl.ds(a, HALF, stride=24), :] = jnp.where(lane48 < SITES, even_re, even_im)
        result[pl.ds(8 + a, HALF, stride=24), :] = jnp.where(lane48 < 64, even_im, odd_re)
        result[pl.ds(16 + a, HALF, stride=24), :] = jnp.where(lane48 < 32, odd_re, odd_im)
    sent(tag_in_tiles, 1, 0, has_lower)
    sent(up_in_tiles, 2 * PIECES, 1, has_lower)
    sent(reply_in_tiles, 2 * PIECES, 2, has_upper)


def on_device(
    section_state,
    coupling,
    site_energy,
    bath_rate,
    bath_strength,
    bath_of_site,
    quanta,
    send_list,
    dest_slot,
):
    slots, width = section_state.shape
    chunks = width // LANES
    tiled = section_state.reshape(slots, chunks, LANES).transpose(1, 0, 2).reshape(-1, LANES)
    operands = (
        tiled,
        coupling,
        site_energy.reshape(1, SITES),
        bath_rate.reshape(1, SITES),
        bath_strength.reshape(1, SITES),
        bath_of_site.reshape(1, SITES),
        quanta.T,
        send_list,
        dest_slot,
    )
    tile_buffer = pltpu.VMEM((TILES * 8, LANES), F32)
    out = pl.pallas_call(
        kernel,
        out_shape=pltpu.VMEM(tiled.shape, F32),
        in_specs=[pl.BlockSpec(memory_space=pltpu.HBM)] * 9,
        out_specs=pl.BlockSpec(memory_space=pltpu.VMEM),
        scratch_shapes=[
            pltpu.VMEM(tiled.shape, F32),
            pltpu.VMEM((SITES, SITES), F32),
            pltpu.VMEM((3, 1, SITES), F32),
            pltpu.VMEM((1, SITES), jnp.int32),
            pltpu.VMEM((DEPTH, SLOTS), jnp.int32),
            pltpu.VMEM((1, LANES), jnp.int32),
            pltpu.VMEM((1, LANES), jnp.int32),
            tile_buffer,
            tile_buffer,
            tile_buffer,
            tile_buffer,
            tile_buffer,
            tile_buffer,
            pltpu.VMEM((LANES, LANES), F32),
            pltpu.VMEM((LANES, LANES), F32),
            pltpu.VMEM((SLOTS * LANES, 2 * LANES), BF16),
            pltpu.VMEM((SLOTS * LANES, 2 * LANES), BF16),
            pltpu.VMEM((2 * SLOTS * SITES, LANES), F32),
            pltpu.VMEM((SLOTS * SITES, 2 * PIECES * LANES), BF16),
            pltpu.VMEM((SLOTS * SITES, 2 * LANES), F32),
            pltpu.SemaphoreType.DMA,
            pltpu.SemaphoreType.DMA((8,)),
            pltpu.SemaphoreType.DMA((3,)),
            pltpu.SemaphoreType.DMA((6,)),
        ],
        compiler_params=pltpu.CompilerParams(
            collective_id=0, has_side_effects=True, vmem_limit_bytes=32 * 1024 * 1024
        ),
    )(*[pltpu.with_memory_space_constraint(value, pltpu.HBM) for value in operands])
    return out.reshape(chunks, slots, LANES).transpose(1, 0, 2).reshape(slots, width)


def solution(mesh):
    return jax.shard_map(
        on_device,
        mesh=mesh,
        in_specs=(
            P(("tier", "aux"), None),
            P(),
            P(),
            P(),
            P(),
            P(),
            P(("tier", "aux"), None),
            P(("tier", "aux"), None),
            P(("tier", "aux"), None),
        ),
        out_specs=P(("tier", "aux"), None),
        check_vma=False,
    )
```
